256 devices in a mesh: tm: 8 (over x, core), space: 32 (over y, z).
Axes of the slice: x: 4, y: 4, z: 8, core: 2. Of those that a mesh axis runs over, the one named last changes fastest.
Arguments:
- state: bfloat16 [32, 5, 1280, 1024], P('tm', None, 'space'), may hold values from -2 to 8, as said below
- spectral: bfloat16 [32, 32], replicated, may hold values from -1 to 1
- deriv_i: bfloat16 [1024, 1024], replicated, may hold values from -0.1875 to 0.1875
- deriv_j: bfloat16 [1280, 1280], replicated, may hold values from -0.15625 to 0.15625
- metric_i: float32 [3, 1280, 1024], P(None, 'space'), may hold values from 0.3 to 1.5
- metric_j: float32 [3, 1280, 1024], P(None, 'space'), may hold values from 0.3 to 1.5
Outputs:
- residual: bfloat16 [32, 5, 1280, 1024], P('tm', None, 'space')
The draws below stay inside these ranges and needn't reach their ends.
Inputs may be any that keep to these rules, and one draw needn't show every extreme that they name: `state`: each cell holds density between 0.6 and 1.6, speeds under 1.3 in each component and pressure between 0.5 and 2, in conserved form.
All inputs are finite; a program needn't handle non-finite values.
Results may differ from the reference program's by a relative error of at most 0.0047.
Values may be sent and summed in bfloat16 or wider, within the bound.
No kernel may reach another device: no remote copies, remote signals or barrier semaphores. Data moves between devices by JAX's collectives and lax.ppermute only.
A program may use at most 128 MiB of HBM per device.

```python
import math
import jax
import jax.numpy as jnp
from jax import lax

NT = 32
NV = 5
NI = 1024
NJ = 1280


def draw_state(key, part):
    key = jax.random.fold_in(key, 7)
    key_rho, key_vel, key_press = jax.random.split(key, 3)
    shape = (NT, NJ, NI)
    rho = jax.random.uniform(key_rho, shape, jnp.float32, 0.7, 1.4)
    velocity = 0.35 * jax.random.truncated_normal(key_vel, -2.0, 2.0, (3,) + shape, jnp.float32)
    pressure = jax.random.uniform(key_press, shape, jnp.float32, 0.6, 1.6)
    energy = pressure / 0.4 + 0.5 * rho * jnp.sum(velocity * velocity, axis=0)
    cons = jnp.stack([rho, rho * velocity[0], rho * velocity[1], rho * velocity[2], energy], axis=1)
    return cons.astype(jnp.bfloat16)


def block_levels(rng, dims, shards, low, high):
    level = 1.0
    for dim, parts in shards:
        draws = jax.random.uniform(jax.random.fold_in(jax.random.fold_in(rng, 6), dim), (parts,), jnp.float32, low / len(shards), high / len(shards))
        level = level * jnp.repeat(jnp.exp(draws), dims[dim] // parts).reshape((-1,) + (1,) * (len(dims) - 1 - dim))
    return level


def normal_values(stream_key, dims, deviation, limit, held_as=jnp.bfloat16):
    drawn = jax.random.normal(stream_key, dims, jnp.float32) * deviation
    return jnp.minimum(jnp.maximum(drawn, -limit), limit).astype(held_as)


def setup_inputs(seed: int = 0) -> dict:
    splits = jax.random.split(jax.random.key(seed), 7)
    return {
        "state": draw_state(jax.random.fold_in(splits[6], 71), 0),
        "spectral": normal_values(splits[1], (NT, NT), NT ** -0.5, 1.0),
        "deriv_i": normal_values(splits[2], (NI, NI), NI ** -0.5, 0.1875),
        "deriv_j": normal_values(splits[3], (NJ, NJ), NJ ** -0.5, 0.15625),
        "metric_i": jnp.clip(jnp.exp(math.log(1.5) - 1.60943787 * jax.random.uniform(splits[4], (3, NJ, NI), jnp.float32) ** block_levels(splits[4], (3, NJ, NI), ((1, 32),), -0.2, 0.2)), 0.3, 1.5),
        "metric_j": jnp.clip(jnp.exp(math.log(1.5) - 1.60943787 * jax.random.uniform(splits[5], (3, NJ, NI), jnp.float32) ** block_levels(splits[5], (3, NJ, NI), ((1, 32),), -0.2, 0.2)), 0.3, 1.5),
    }


def rusanov_parts(cons, metric):
    rho = cons[:, 0]
    velocity = cons[:, 1:4] / rho[:, None]
    energy = cons[:, 4]
    pressure = 0.4 * (energy - 0.5 * rho * lax.optimization_barrier(jnp.sum(velocity * velocity, axis=1)))
    contra = lax.optimization_barrier(jnp.sum(metric[None] * velocity, axis=1))
    flux = jnp.stack([rho * contra, cons[:, 1] * contra + metric[0][None] * pressure, cons[:, 2] * contra + metric[1][None] * pressure, cons[:, 3] * contra + metric[2][None] * pressure, (energy + pressure) * contra], axis=1)
    radius = jnp.abs(contra) + jnp.sqrt(1.4 * pressure / rho * lax.optimization_barrier(jnp.sum(metric * metric, axis=0))[None])
    return (flux.astype(jnp.bfloat16), radius)

def second_diff(cons, axis):
    width = [(0, 0)] * cons.ndim
    width[axis] = (1, 1)
    padded = jnp.pad(cons, width)
    size = cons.shape[axis]
    upper = lax.slice_in_dim(padded, 2, size + 2, axis=axis)
    lower = lax.slice_in_dim(padded, 0, size, axis=axis)
    return upper + lower - 2.0 * cons

def reference(state, spectral, deriv_i, deriv_j, metric_i, metric_j):
    flat = state.reshape(NT, -1)

    def one_instance(pair):
        row, cons_b = pair
        source = jnp.dot(row[None], flat, preferred_element_type=jnp.float32).reshape(1, NV, NJ, NI)
        cons = cons_b[None].astype(jnp.float32)
        flux_i, radius_i = rusanov_parts(cons, metric_i)
        term_i = jnp.dot(flux_i.reshape(-1, NI), deriv_i.T, preferred_element_type=jnp.float32).reshape(1, NV, NJ, NI)
        term_i = term_i - 0.25 * radius_i[:, None] * second_diff(cons, 3)
        flux_j, radius_j = rusanov_parts(cons, metric_j)
        slope_j = jnp.einsum('kj,tvji->tvki', deriv_j.astype(jnp.float32), flux_j.astype(jnp.float32)).astype(jnp.bfloat16)
        total = source + term_i + slope_j.astype(jnp.float32) - 0.25 * radius_j[:, None] * second_diff(cons, 2)
        return total[0].astype(jnp.bfloat16)
    return lax.map(one_instance, (spectral, state))
```

```python
import jax
import jax.numpy as jnp
from jax import lax
from jax.experimental import pallas as pl
from jax.experimental.pallas import tpu as pltpu
from jax.sharding import PartitionSpec as P

LANES = 128
VMEM_LIMIT = 40 * 1024 * 1024


def primitives(cons, metric):
    rho, mx, my, mz, energy = cons
    ax, ay, az = metric
    inv = 1.0 / rho
    contra = (ax * mx + ay * my + az * mz) * inv
    pressure = 0.4 * (energy - 0.5 * (mx * mx + my * my + mz * mz) * inv)
    return inv, contra, pressure


def flux_of(cons, metric, contra, pressure):
    rho, mx, my, mz, energy = cons
    ax, ay, az = metric
    return (
        rho * contra,
        mx * contra + ax * pressure,
        my * contra + ay * pressure,
        mz * contra + az * pressure,
        (energy + pressure) * contra,
    )


def radius_of(metric, inv, contra, pressure):
    ax, ay, az = metric
    return jnp.abs(contra) + jnp.sqrt(1.4 * pressure * inv * (ax * ax + ay * ay + az * az))


def flux_j_kernel(state_ref, metric_ref, out_ref):
    blocks = state_ref.shape[3] // LANES
    for b in range(blocks):
        cols = slice(b * LANES, (b + 1) * LANES)
        cons = [state_ref[0, v, :, cols].astype(jnp.float32) for v in range(5)]
        metric = [metric_ref[c, :, cols] for c in range(3)]
        _, contra, pressure = primitives(cons, metric)
        for v, f in enumerate(flux_of(cons, metric, contra, pressure)):
            out_ref[0, b, :, v * LANES : (v + 1) * LANES] = f.astype(jnp.bfloat16)


def flux_j_blocks(state, metric_j):
    nt, nv, nj, ni = state.shape
    blocks = ni // LANES
    return pl.pallas_call(
        flux_j_kernel,
        grid=(nt,),
        out_shape=jax.ShapeDtypeStruct((nt, blocks, nj, nv * LANES), jnp.bfloat16),
        in_specs=[
            pl.BlockSpec((1, nv, nj, ni), lambda t: (t, 0, 0, 0)),
            pl.BlockSpec((3, nj, ni), lambda t: (0, 0, 0)),
        ],
        out_specs=pl.BlockSpec((1, blocks, nj, nv * LANES), lambda t: (t, 0, 0, 0)),
        compiler_params=pltpu.CompilerParams(vmem_limit_bytes=VMEM_LIMIT),
        cost_estimate=pl.CostEstimate(flops=10_000_000, bytes_accessed=4_000_000, transcendentals=200_000),
        name="flux_j",
    )(state, metric_j)


def local_kernel(state_ref, metric_i_ref, metric_j_ref, low_ref, high_ref, deriv_ref, out_ref, flux_ref):
    nv, nj, ni = state_ref.shape[1:]
    metric_i = [metric_i_ref[c] for c in range(3)]
    cons = [state_ref[0, v].astype(jnp.float32) for v in range(nv)]
    inv, contra, pressure = primitives(cons, metric_i)
    for v, f in enumerate(flux_of(cons, metric_i, contra, pressure)):
        flux_ref[v * nj : (v + 1) * nj, :] = f
    radius_i = 0.25 * radius_of(metric_i, inv, contra, pressure)
    metric_j = [metric_j_ref[c] for c in range(3)]
    inv, contra, pressure = primitives(cons, metric_j)
    radius_j = 0.25 * radius_of(metric_j, inv, contra, pressure)
    term = lax.dot_general(
        flux_ref[...].astype(jnp.bfloat16),
        deriv_ref[...],
        (((1,), (1,)), ((), ())),
        preferred_element_type=jnp.float32,
    )
    row = lax.broadcasted_iota(jnp.int32, (nj, ni), 0)
    col = lax.broadcasted_iota(jnp.int32, (nj, ni), 1)
    low = low_ref[0].astype(jnp.float32)
    high = high_ref[0].astype(jnp.float32)
    for v in range(nv):
        c = cons[v]
        right = jnp.where(col == ni - 1, 0.0, pltpu.roll(c, ni - 1, 1))
        left = jnp.where(col == 0, 0.0, pltpu.roll(c, 1, 1))
        up = jnp.where(row == nj - 1, high[v : v + 1], pltpu.roll(c, nj - 1, 0))
        down = jnp.where(row == 0, low[v : v + 1], pltpu.roll(c, 1, 0))
        twice = 2.0 * c
        damping = radius_i * (right + left - twice) + radius_j * (up + down - twice)
        out_ref[0, v] = term[v * nj : (v + 1) * nj] - damping


def local_terms(state, metric_i, metric_j, low, high, deriv_i):
    nt, nv, nj, ni = state.shape
    whole3 = pl.BlockSpec((3, nj, ni), lambda t: (0, 0, 0))
    halo = pl.BlockSpec((1, nv, ni), lambda t: (t, 0, 0))
    per_t = pl.BlockSpec((1, nv, nj, ni), lambda t: (t, 0, 0, 0))
    return pl.pallas_call(
        local_kernel,
        grid=(nt,),
        out_shape=jax.ShapeDtypeStruct((nt, nv, nj, ni), jnp.float32),
        in_specs=[per_t, whole3, whole3, halo, halo, pl.BlockSpec((ni, ni), lambda t: (0, 0))],
        out_specs=per_t,
        scratch_shapes=[pltpu.VMEM((nv * nj, ni), jnp.float32)],
        compiler_params=pltpu.CompilerParams(vmem_limit_bytes=VMEM_LIMIT),
        cost_estimate=pl.CostEstimate(
            flops=2 * nt * nv * nj * ni * ni, bytes_accessed=9_000_000, transcendentals=600_000
        ),
        name="local_terms",
    )(state, metric_i, metric_j, low, high, deriv_i)


def slope_kernel(deriv_ref, lines_ref, out_ref):
    out_ref[...] = jnp.dot(
        deriv_ref[...], lines_ref[...], preferred_element_type=jnp.float32
    ).astype(jnp.bfloat16)


def slope_lines(deriv_j, lines):
    size, width = lines.shape
    rows = 256
    return pl.pallas_call(
        slope_kernel,
        grid=(size // rows,),
        out_shape=jax.ShapeDtypeStruct((size, width), jnp.bfloat16),
        in_specs=[
            pl.BlockSpec((rows, size), lambda k: (k, 0)),
            pl.BlockSpec((size, width), lambda k: (0, 0)),
        ],
        out_specs=pl.BlockSpec((rows, width), lambda k: (k, 0)),
        compiler_params=pltpu.CompilerParams(vmem_limit_bytes=VMEM_LIMIT),
        cost_estimate=pl.CostEstimate(
            flops=2 * size * size * width, bytes_accessed=7_000_000, transcendentals=0
        ),
        name="slope_lines",
    )(deriv_j, lines)


def finish_kernel(total_ref, slope_ref, out_ref):
    nv = total_ref.shape[1]
    for b in range(slope_ref.shape[1]):
        cols = slice(b * LANES, (b + 1) * LANES)
        for v in range(nv):
            s = slope_ref[0, b, :, v * LANES : (v + 1) * LANES].astype(jnp.float32)
            out_ref[0, v, :, cols] = (total_ref[0, v, :, cols] + s).astype(jnp.bfloat16)


def finish(total, slope):
    nt, nv, nj, ni = total.shape
    per_t = pl.BlockSpec((1, nv, nj, ni), lambda t: (t, 0, 0, 0))
    return pl.pallas_call(
        finish_kernel,
        grid=(nt,),
        out_shape=jax.ShapeDtypeStruct((nt, nv, nj, ni), jnp.bfloat16),
        in_specs=[per_t, pl.BlockSpec((1,) + slope.shape[1:], lambda t: (t, 0, 0, 0))],
        out_specs=per_t,
        compiler_params=pltpu.CompilerParams(vmem_limit_bytes=VMEM_LIMIT),
        cost_estimate=pl.CostEstimate(flops=1_000_000, bytes_accessed=7_000_000, transcendentals=0),
        name="finish",
    )(total, slope)


def on_device(state, spectral, deriv_i, deriv_j, metric_i, metric_j):
    nt, nv, nj, ni = state.shape
    count = lax.axis_size("space")
    forward = [(i, i + 1) for i in range(count - 1)]
    backward = [(target, source) for source, target in forward]
    gathered = lax.all_gather(state, "tm", axis=0, tiled=True)
    low = lax.ppermute(state[:, :, nj - 1, :], "space", forward)
    high = lax.ppermute(state[:, :, 0, :], "space", backward)
    outgoing = flux_j_blocks(state, metric_j).reshape(count, nj, nv * LANES)
    lines = lax.all_to_all(outgoing, "space", split_axis=0, concat_axis=0, tiled=True)
    lines, low, high = lax.optimization_barrier((lines, low, high))
    partial = local_terms(state, metric_i, metric_j, low, high, deriv_i)
    slope = slope_lines(deriv_j, lines.reshape(count * nj, nv * LANES))
    slope = lax.all_to_all(
        slope.reshape(count, nj, nv * LANES), "space", split_axis=0, concat_axis=0, tiled=True
    )
    own_rows = lax.dynamic_slice_in_dim(spectral, lax.axis_index("tm") * nt, nt, 0)
    source = jnp.einsum("nm,mvji->nvji", own_rows, gathered, preferred_element_type=jnp.float32)
    total = source + partial
    return finish(total, slope.reshape(nt, ni // LANES, nj, nv * LANES))


def solution(mesh):
    return jax.shard_map(
        on_device,
        mesh=mesh,
        in_specs=(
            P("tm", None, "space", None),
            P(),
            P(),
            P(),
            P(None, "space", None),
            P(None, "space", None),
        ),
        out_specs=P("tm", None, "space", None),
        check_vma=False,
    )
```

```python
import jax
import jax.numpy as jnp
from jax import lax
from jax.experimental import pallas as pl
from jax.experimental.pallas import tpu as pltpu
from jax.sharding import PartitionSpec as P

LANES = 128
VMEM_LIMIT = 40 * 1024 * 1024


def primitives(cons, metric):
    rho, mx, my, mz, energy = cons
    ax, ay, az = metric
    inv = 1.0 / rho
    contra = (ax * mx + ay * my + az * mz) * inv
    pressure = 0.4 * (energy - 0.5 * (mx * mx + my * my + mz * mz) * inv)
    return inv, contra, pressure


def flux_of(cons, metric, contra, pressure):
    rho, mx, my, mz, energy = cons
    ax, ay, az = metric
    return (
        rho * contra,
        mx * contra + ax * pressure,
        my * contra + ay * pressure,
        mz * contra + az * pressure,
        (energy + pressure) * contra,
    )


def radius_of(metric, inv, contra, pressure):
    ax, ay, az = metric
    return jnp.abs(contra) + jnp.sqrt(1.4 * pressure * inv * (ax * ax + ay * ay + az * az))


def flux_j_kernel(state_hbm, metric_hbm, out_hbm, state_ref, metric_ref, out_ref, in_sems, out_sems):
    nt = state_ref.shape[0]
    blocks = out_ref.shape[1]
    half = blocks // 2
    metric_copy = pltpu.make_async_copy(metric_hbm, metric_ref, in_sems.at[nt])
    metric_copy.start()
    copies = [
        pltpu.make_async_copy(state_hbm.at[t], state_ref.at[t], in_sems.at[t]) for t in range(nt)
    ]
    for copy in copies:
        copy.start()
    metric_copy.wait()
    sent = []
    for t in range(nt):
        copies[t].wait()
        for b in range(blocks):
            cols = slice(b * LANES, (b + 1) * LANES)
            cons = [state_ref[t, v, :, cols].astype(jnp.float32) for v in range(5)]
            metric = [metric_ref[c, :, cols] for c in range(3)]
            _, contra, pressure = primitives(cons, metric)
            for v, f in enumerate(flux_of(cons, metric, contra, pressure)):
                out_ref[t, b, :, v * LANES : (v + 1) * LANES] = f.astype(jnp.bfloat16)
            if (b + 1) % half == 0:
                part = pl.ds(b + 1 - half, half)
                copy = pltpu.make_async_copy(
                    out_ref.at[t, part], out_hbm.at[t, part], out_sems.at[len(sent)]
                )
                copy.start()
                sent.append(copy)
    for copy in sent:
        copy.wait()


def in_hbm(x):
    return pltpu.with_memory_space_constraint(x, pltpu.HBM)


def flux_j_blocks(state, metric_j):
    nt, nv, nj, ni = state.shape
    blocks = ni // LANES
    hbm = pl.BlockSpec(memory_space=pltpu.HBM)
    shape = (nt, blocks, nj, nv * LANES)
    return pl.pallas_call(
        flux_j_kernel,
        out_shape=pltpu.HBM(shape, jnp.bfloat16),
        in_specs=[hbm, hbm],
        out_specs=hbm,
        scratch_shapes=[
            pltpu.VMEM(state.shape, jnp.bfloat16),
            pltpu.VMEM(metric_j.shape, jnp.float32),
            pltpu.VMEM(shape, jnp.bfloat16),
            pltpu.SemaphoreType.DMA((nt + 1,)),
            pltpu.SemaphoreType.DMA((2 * nt,)),
        ],
        compiler_params=pltpu.CompilerParams(vmem_limit_bytes=VMEM_LIMIT),
        cost_estimate=pl.CostEstimate(flops=10_000_000, bytes_accessed=4_000_000, transcendentals=200_000),
        name="flux_j",
    )(in_hbm(state), in_hbm(metric_j))


def pack_kernel(me_ref, state_ref, first_ref, last_ref, *outs):
    nv, nj = state_ref.shape[1:3]
    for k, out in enumerate(outs):
        cols = pl.ds(pl.multiple_of((me_ref[0] ^ k) * LANES, LANES), LANES)
        for v in range(nv):
            out[0, v] = state_ref[0, v, :, cols]
    cons = [state_ref[0, v].astype(jnp.float32) for v in range(nv)]
    first_ref[0] = jnp.concatenate([c[:1] for c in cons], axis=0).astype(jnp.bfloat16)
    last_ref[0] = jnp.concatenate([c[nj - 1 :] for c in cons], axis=0).astype(jnp.bfloat16)


def pack_blocks(me, state):
    nt, nv, nj, ni = state.shape
    peers = ni // LANES
    block = pl.BlockSpec((1, nv, nj, LANES), lambda t: (t, 0, 0, 0))
    edge = pl.BlockSpec((1, nv, ni), lambda t: (t, 0, 0))
    first, last, *blocks = pl.pallas_call(
        pack_kernel,
        grid=(nt,),
        out_shape=[pltpu.HBM((nt, nv, ni), state.dtype)] * 2
        + [pltpu.HBM((nt, nv, nj, LANES), state.dtype)] * peers,
        in_specs=[
            pl.BlockSpec(memory_space=pltpu.SMEM),
            pl.BlockSpec((1, nv, nj, ni), lambda t: (t, 0, 0, 0)),
        ],
        out_specs=[edge] * 2 + [block] * peers,
        compiler_params=pltpu.CompilerParams(vmem_limit_bytes=VMEM_LIMIT),
        cost_estimate=pl.CostEstimate(flops=0, bytes_accessed=3_300_000, transcendentals=0),
        name="pack_blocks",
    )(me, in_hbm(state))
    return first, last, blocks


def source_weights(me, spectral, nt):
    size = spectral.shape[0]
    row = lax.broadcasted_iota(jnp.int32, (size * 8, size), 0)
    col = lax.broadcasted_iota(jnp.int32, (size * 8, size), 1)
    instance = (me ^ (row // (nt * 8))) * nt + (row // 8) % nt
    pick = jnp.where(instance == col, 1.0, 0.0).astype(jnp.bfloat16)
    rows = jnp.dot(pick, spectral, preferred_element_type=jnp.float32).astype(jnp.bfloat16)
    full = lax.dot_general(
        rows, pick, (((1,), (1,)), ((), ())), preferred_element_type=jnp.float32
    )
    r = lax.broadcasted_iota(jnp.int32, full.shape, 0)
    c = lax.broadcasted_iota(jnp.int32, full.shape, 1)
    return jnp.where(r % 8 == c % 8, full, 0.0).astype(jnp.bfloat16)


def source_kernel(me_ref, spectral_ref, deriv_hbm, *refs):
    taken, made, stage, result, in_sems, out_sems, sem = refs[-7:]
    peers = taken.shape[0]
    ins, outs, held = refs[:peers], refs[peers : 2 * peers], refs[2 * peers]
    fetches = [pltpu.make_async_copy(ins[k], taken.at[k], in_sems.at[k]) for k in range(peers)]
    for copy in fetches:
        copy.start()
    fetch = pltpu.make_async_copy(deriv_hbm, held, sem)
    fetch.start()
    nt, nv, nj = taken.shape[1:4]
    tiles = nj // 8
    weights = source_weights(me_ref[0], spectral_ref[...], nt)
    for k in range(peers):
        fetches[k].wait()
        for t in range(nt):
            m = k * nt + t
            for v in range(nv):
                x = taken[k, t, v].astype(jnp.float32)
                for b in range(tiles):
                    stage[b, m * 8 : (m + 1) * 8, v * LANES : (v + 1) * LANES] = x[b * 8 : (b + 1) * 8]
    for b in range(tiles):
        result[b] = jnp.dot(
            weights, stage[b].astype(jnp.bfloat16), preferred_element_type=jnp.float32
        )
    sent = []
    for k in range(peers):
        for t in range(nt):
            n = k * nt + t
            for v in range(nv):
                parts = [
                    result[b, n * 8 : (n + 1) * 8, v * LANES : (v + 1) * LANES] for b in range(tiles)
                ]
                made[k, t, v] = jnp.concatenate(parts, axis=0).astype(jnp.bfloat16)
        copy = pltpu.make_async_copy(made.at[k], outs[k], out_sems.at[k])
        copy.start()
        sent.append(copy)
    for copy in sent:
        copy.wait()
    fetch.wait()


def source_blocks(me, spectral, deriv_j, blocks):
    shape = blocks[0].shape
    nt, nv, nj, _ = shape
    peers = len(blocks)
    rows = peers * nt * 8
    vmem = pl.BlockSpec(memory_space=pltpu.VMEM)
    hbm = pl.BlockSpec(memory_space=pltpu.HBM)
    *sources, held = pl.pallas_call(
        source_kernel,
        out_shape=[pltpu.HBM(shape, jnp.bfloat16)] * peers
        + [pltpu.VMEM(deriv_j.shape, deriv_j.dtype)],
        in_specs=[pl.BlockSpec(memory_space=pltpu.SMEM), vmem, hbm] + [hbm] * peers,
        out_specs=[hbm] * peers + [vmem],
        scratch_shapes=[pltpu.VMEM((peers,) + shape, jnp.bfloat16)] * 2
        + [pltpu.VMEM((nj // 8, rows, nv * LANES), jnp.float32)] * 2
        + [pltpu.SemaphoreType.DMA((peers,))] * 2
        + [pltpu.SemaphoreType.DMA],
        compiler_params=pltpu.CompilerParams(vmem_limit_bytes=VMEM_LIMIT),
        cost_estimate=pl.CostEstimate(flops=420_000_000, bytes_accessed=10_000_000, transcendentals=0),
        name="source_blocks",
    )(me, spectral, in_hbm(deriv_j), *[in_hbm(b) for b in blocks])
    return sources, held


def local_kernel(
    me_ref, state_ref, metric_i_ref, metric_j_ref, low_ref, high_ref, deriv_ref, *refs
):
    sources, out_ref, flux_ref = refs[:-2], refs[-2], refs[-1]
    nv, nj, ni = state_ref.shape[1:]
    metric_i = [metric_i_ref[c] for c in range(3)]
    cons = [state_ref[0, v].astype(jnp.float32) for v in range(nv)]
    inv, contra, pressure = primitives(cons, metric_i)
    for v, f in enumerate(flux_of(cons, metric_i, contra, pressure)):
        flux_ref[v * nj : (v + 1) * nj, :] = f
    radius_i = 0.25 * radius_of(metric_i, inv, contra, pressure)
    metric_j = [metric_j_ref[c] for c in range(3)]
    inv, contra, pressure = primitives(cons, metric_j)
    radius_j = 0.25 * radius_of(metric_j, inv, contra, pressure)
    term = lax.dot_general(
        flux_ref[...].astype(jnp.bfloat16),
        deriv_ref[...],
        (((1,), (1,)), ((), ())),
        preferred_element_type=jnp.float32,
    )
    row = lax.broadcasted_iota(jnp.int32, (nj, ni), 0)
    col = lax.broadcasted_iota(jnp.int32, (nj, ni), 1)
    low = low_ref[0].astype(jnp.float32)
    high = high_ref[0].astype(jnp.float32)
    for v in range(nv):
        c = cons[v]
        right = jnp.where(col == ni - 1, 0.0, pltpu.roll(c, ni - 1, 1))
        left = jnp.where(col == 0, 0.0, pltpu.roll(c, 1, 1))
        up = jnp.where(row == nj - 1, high[v : v + 1], pltpu.roll(c, nj - 1, 0))
        down = jnp.where(row == 0, low[v : v + 1], pltpu.roll(c, 1, 0))
        twice = 2.0 * c
        damping = radius_i * (right + left - twice) + radius_j * (up + down - twice)
        out_ref[0, v] = term[v * nj : (v + 1) * nj] - damping
    for k, source_ref in enumerate(sources):
        cols = pl.ds(pl.multiple_of((me_ref[0] ^ k) * LANES, LANES), LANES)
        for v in range(nv):
            out_ref[0, v, :, cols] += source_ref[0, v].astype(jnp.float32)


def local_terms(me, state, metric_i, metric_j, low, high, deriv_i, sources):
    nt, nv, nj, ni = state.shape
    whole3 = pl.BlockSpec((3, nj, ni), lambda t: (0, 0, 0))
    halo = pl.BlockSpec((1, nv, ni), lambda t: (t, 0, 0))
    per_t = pl.BlockSpec((1, nv, nj, ni), lambda t: (t, 0, 0, 0))
    block = pl.BlockSpec((1, nv, nj, LANES), lambda t: (t, 0, 0, 0))
    return pl.pallas_call(
        local_kernel,
        grid=(nt,),
        out_shape=pltpu.VMEM((nt, nv, nj, ni), jnp.float32),
        in_specs=[
            pl.BlockSpec(memory_space=pltpu.SMEM),
            per_t,
            whole3,
            whole3,
            halo,
            halo,
            pl.BlockSpec((ni, ni), lambda t: (0, 0)),
        ]
        + [block] * len(sources),
        out_specs=per_t,
        scratch_shapes=[pltpu.VMEM((nv * nj, ni), jnp.float32)],
        compiler_params=pltpu.CompilerParams(vmem_limit_bytes=VMEM_LIMIT),
        cost_estimate=pl.CostEstimate(
            flops=2 * nt * nv * nj * ni * ni, bytes_accessed=11_000_000, transcendentals=600_000
        ),
        name="local_terms",
    )(me, *[in_hbm(x) for x in (state, metric_i, metric_j, low, high, deriv_i, *sources)])


ROWS = 256


def slope_kernel(deriv_ref, lines_hbm, out_hbm, lines_ref, out_ref, in_sems, out_sems):
    chunks = out_ref.shape[0] // ROWS
    pieces = [pl.ds(c * ROWS, ROWS) for c in range(chunks)]
    fetches = [
        pltpu.make_async_copy(lines_hbm.at[p], lines_ref.at[p], in_sems.at[c])
        for c, p in enumerate(pieces)
    ]
    for copy in fetches:
        copy.start()
    copies = []
    for c, rows in enumerate(pieces):
        if c == 0:
            total = None
            for d, p in enumerate(pieces):
                fetches[d].wait()
                part = jnp.dot(
                    deriv_ref[rows, d * ROWS : (d + 1) * ROWS],
                    lines_ref[p, :],
                    preferred_element_type=jnp.float32,
                )
                total = part if total is None else total + part
        else:
            total = jnp.dot(deriv_ref[rows, :], lines_ref[...], preferred_element_type=jnp.float32)
        out_ref[rows, :] = total.astype(jnp.bfloat16)
        copy = pltpu.make_async_copy(out_ref.at[rows], out_hbm.at[rows], out_sems.at[c])
        copy.start()
        copies.append(copy)
    for copy in copies:
        copy.wait()


def slope_lines(deriv_j, lines):
    size, width = lines.shape
    hbm = pl.BlockSpec(memory_space=pltpu.HBM)
    return pl.pallas_call(
        slope_kernel,
        out_shape=pltpu.HBM((size, width), jnp.bfloat16),
        in_specs=[pl.BlockSpec(memory_space=pltpu.VMEM), hbm],
        out_specs=hbm,
        scratch_shapes=[pltpu.VMEM((size, width), jnp.bfloat16)] * 2
        + [pltpu.SemaphoreType.DMA((size // ROWS,))] * 2,
        compiler_params=pltpu.CompilerParams(vmem_limit_bytes=VMEM_LIMIT),
        cost_estimate=pl.CostEstimate(
            flops=2 * size * size * width, bytes_accessed=7_000_000, transcendentals=0
        ),
        name="slope_lines",
    )(deriv_j, in_hbm(lines))


def finish_kernel(total_ref, slope_hbm, out_hbm, slope_ref, out_ref, in_sems, out_sems):
    nt, nv = total_ref.shape[:2]
    copies = [
        pltpu.make_async_copy(slope_hbm.at[t], slope_ref.at[t], in_sems.at[t]) for t in range(nt)
    ]
    for copy in copies:
        copy.start()
    sent = []
    for t in range(nt):
        copies[t].wait()
        for b in range(slope_ref.shape[1]):
            cols = slice(b * LANES, (b + 1) * LANES)
            for v in range(nv):
                s = slope_ref[t, b, :, v * LANES : (v + 1) * LANES].astype(jnp.float32)
                out_ref[t, v, :, cols] = (total_ref[t, v, :, cols] + s).astype(jnp.bfloat16)
        copy = pltpu.make_async_copy(out_ref.at[t], out_hbm.at[t], out_sems.at[t])
        copy.start()
        sent.append(copy)
    for copy in sent:
        copy.wait()


def finish(total, slope):
    nt = total.shape[0]
    hbm = pl.BlockSpec(memory_space=pltpu.HBM)
    return pl.pallas_call(
        finish_kernel,
        out_shape=jax.ShapeDtypeStruct(total.shape, jnp.bfloat16),
        in_specs=[pl.BlockSpec(memory_space=pltpu.VMEM), hbm],
        out_specs=hbm,
        scratch_shapes=[
            pltpu.VMEM(slope.shape, jnp.bfloat16),
            pltpu.VMEM(total.shape, jnp.bfloat16),
            pltpu.SemaphoreType.DMA((nt,)),
            pltpu.SemaphoreType.DMA((nt,)),
        ],
        compiler_params=pltpu.CompilerParams(vmem_limit_bytes=VMEM_LIMIT),
        cost_estimate=pl.CostEstimate(flops=1_000_000, bytes_accessed=7_000_000, transcendentals=0),
        name="finish",
    )(total, in_hbm(slope))


def on_device(state, spectral, deriv_i, deriv_j, metric_i, metric_j):
    nt, nv, nj, ni = state.shape
    count = lax.axis_size("space")
    forward = [(i, i + 1) for i in range(count - 1)]
    backward = [(target, source) for source, target in forward]
    peers = lax.axis_size("tm")
    swaps = [[(i, i ^ k) for i in range(peers)] for k in range(peers)]
    rank = lax.axis_index("tm")
    me = jnp.reshape(rank, (1,)).astype(jnp.int32)
    outgoing = flux_j_blocks(state, metric_j).reshape(count, nj, nv * LANES)
    lines = lax.all_to_all(outgoing, "space", split_axis=0, concat_axis=0, tiled=True)
    first, last, own = pack_blocks(me, state)
    low = lax.ppermute(last, "space", forward)
    high = lax.ppermute(first, "space", backward)
    blocks = own[:1] + [lax.ppermute(own[k], "tm", swaps[k]) for k in range(1, peers)]
    sources, held = source_blocks(me, spectral, deriv_j, blocks)
    lines, low, high = lax.optimization_barrier((lines, low, high))
    sources = sources[:1] + [lax.ppermute(sources[k], "tm", swaps[k]) for k in range(1, peers)]
    partial = local_terms(me, state, metric_i, metric_j, low, high, deriv_i, sources)
    slope = slope_lines(held, lines.reshape(count * nj, nv * LANES))
    slope = lax.all_to_all(
        slope.reshape(count, nj, nv * LANES), "space", split_axis=0, concat_axis=0, tiled=True
    )
    return finish(partial, slope.reshape(nt, ni // LANES, nj, nv * LANES))


def solution(mesh):
    return jax.shard_map(
        on_device,
        mesh=mesh,
        in_specs=(
            P("tm", None, "space", None),
            P(),
            P(),
            P(),
            P(None, "space", None),
            P(None, "space", None),
        ),
        out_specs=P("tm", None, "space", None),
        check_vma=False,
    )
```

```python
import jax
import jax.numpy as jnp
from jax import lax
from jax.experimental import pallas as pl
from jax.experimental.pallas import tpu as pltpu
from jax.sharding import PartitionSpec as P

LANES = 128
VMEM_LIMIT = 28 * 1024 * 1024
VMEM_SMALL = 12 * 1024 * 1024


def primitives(cons, metric):
    rho, mx, my, mz, energy = cons
    ax, ay, az = metric
    inv = 1.0 / rho
    contra = (ax * mx + ay * my + az * mz) * inv
    pressure = 0.4 * (energy - 0.5 * (mx * mx + my * my + mz * mz) * inv)
    return inv, contra, pressure


def flux_of(cons, metric, contra, pressure):
    rho, mx, my, mz, energy = cons
    ax, ay, az = metric
    return (
        rho * contra,
        mx * contra + ax * pressure,
        my * contra + ay * pressure,
        mz * contra + az * pressure,
        (energy + pressure) * contra,
    )


def radius_of(metric, inv, contra, pressure):
    ax, ay, az = metric
    return jnp.abs(contra) + jnp.sqrt(1.4 * pressure * inv * (ax * ax + ay * ay + az * az))


def flux_j_kernel(state_hbm, metric_hbm, out_hbm, state_ref, metric_ref, out_ref, in_sems, out_sems):
    nt = state_ref.shape[0]
    blocks = out_ref.shape[1]
    metric_copy = pltpu.make_async_copy(metric_hbm, metric_ref, in_sems.at[nt])
    metric_copy.start()
    copies = [
        pltpu.make_async_copy(state_hbm.at[t], state_ref.at[t], in_sems.at[t]) for t in range(nt)
    ]
    for copy in copies:
        copy.start()
    metric_copy.wait()

    @pl.loop(0, nt)
    def _(t):
        pltpu.make_async_copy(state_hbm.at[t], state_ref.at[t], in_sems.at[t]).wait()
        for b in range(blocks):
            cols = slice(b * LANES, (b + 1) * LANES)
            cons = [state_ref[t, v, :, cols].astype(jnp.float32) for v in range(5)]
            metric = [metric_ref[c, :, cols] for c in range(3)]
            _, contra, pressure = primitives(cons, metric)
            for v, f in enumerate(flux_of(cons, metric, contra, pressure)):
                out_ref[t, b, :, v * LANES : (v + 1) * LANES] = f.astype(jnp.bfloat16)
        pltpu.make_async_copy(out_ref.at[t], out_hbm.at[t], out_sems.at[t]).start()

    @pl.loop(0, nt)
    def _(t):
        pltpu.make_async_copy(out_ref.at[t], out_hbm.at[t], out_sems.at[t]).wait()


def in_hbm(x):
    return pltpu.with_memory_space_constraint(x, pltpu.HBM)


def flux_j_blocks(state, metric_j):
    nt, nv, nj, ni = state.shape
    blocks = ni // LANES
    hbm = pl.BlockSpec(memory_space=pltpu.HBM)
    shape = (nt, blocks, nj, nv * LANES)
    return pl.pallas_call(
        flux_j_kernel,
        out_shape=pltpu.HBM(shape, jnp.bfloat16),
        in_specs=[hbm, hbm],
        out_specs=hbm,
        scratch_shapes=[
            pltpu.VMEM(state.shape, jnp.bfloat16),
            pltpu.VMEM(metric_j.shape, jnp.float32),
            pltpu.VMEM(shape, jnp.bfloat16),
            pltpu.SemaphoreType.DMA((nt + 1,)),
            pltpu.SemaphoreType.DMA((nt,)),
        ],
        compiler_params=pltpu.CompilerParams(vmem_limit_bytes=VMEM_LIMIT),
        cost_estimate=pl.CostEstimate(flops=10_000_000, bytes_accessed=4_000_000, transcendentals=200_000),
        name="flux_j",
    )(in_hbm(state), in_hbm(metric_j))


def pack_kernel(me_ref, state_ref, first_ref, last_ref, *outs):
    nv, nj = state_ref.shape[1:3]
    for k, out in enumerate(outs):
        cols = pl.ds(pl.multiple_of((me_ref[0] ^ k) * LANES, LANES), LANES)
        for v in range(nv):
            out[0, v] = state_ref[0, v, :, cols]
    cons = [state_ref[0, v].astype(jnp.float32) for v in range(nv)]
    first_ref[0] = jnp.concatenate([c[:1] for c in cons], axis=0).astype(jnp.bfloat16)
    last_ref[0] = jnp.concatenate([c[nj - 1 :] for c in cons], axis=0).astype(jnp.bfloat16)


def pack_blocks(me, state):
    nt, nv, nj, ni = state.shape
    peers = ni // LANES
    block = pl.BlockSpec((1, nv, nj, LANES), lambda t: (t, 0, 0, 0))
    edge = pl.BlockSpec((1, nv, ni), lambda t: (t, 0, 0))
    first, last, *blocks = pl.pallas_call(
        pack_kernel,
        grid=(nt,),
        out_shape=[pltpu.HBM((nt, nv, ni), state.dtype)] * 2
        + [pltpu.HBM((nt, nv, nj, LANES), state.dtype)] * peers,
        in_specs=[
            pl.BlockSpec(memory_space=pltpu.SMEM),
            pl.BlockSpec((1, nv, nj, ni), lambda t: (t, 0, 0, 0)),
        ],
        out_specs=[edge] * 2 + [block] * peers,
        compiler_params=pltpu.CompilerParams(vmem_limit_bytes=VMEM_LIMIT),
        cost_estimate=pl.CostEstimate(flops=0, bytes_accessed=3_300_000, transcendentals=0),
        name="pack_blocks",
    )(me, in_hbm(state))
    return first, last, blocks


def source_weights(me, spectral, nt):
    size = spectral.shape[0]
    row = lax.broadcasted_iota(jnp.int32, (size * 8, size), 0)
    col = lax.broadcasted_iota(jnp.int32, (size * 8, size), 1)
    instance = (me ^ (row // (nt * 8))) * nt + (row // 8) % nt
    pick = jnp.where(instance == col, 1.0, 0.0).astype(jnp.bfloat16)
    rows = jnp.dot(pick, spectral, preferred_element_type=jnp.float32).astype(jnp.bfloat16)
    full = lax.dot_general(
        rows, pick, (((1,), (1,)), ((), ())), preferred_element_type=jnp.float32
    )
    r = lax.broadcasted_iota(jnp.int32, full.shape, 0)
    c = lax.broadcasted_iota(jnp.int32, full.shape, 1)
    return jnp.where(r % 8 == c % 8, full, 0.0).astype(jnp.bfloat16)


def source_kernel(me_ref, spectral_ref, deriv_hbm, *refs):
    taken, made, stage, result, in_sems, out_sems, sem = refs[-7:]
    peers = taken.shape[0]
    ins, outs, held = refs[:peers], refs[peers : 2 * peers], refs[2 * peers]
    fetches = [pltpu.make_async_copy(ins[k], taken.at[k], in_sems.at[k]) for k in range(peers)]
    for copy in fetches:
        copy.start()
    fetch = pltpu.make_async_copy(deriv_hbm.at[pl.ds(0, held.shape[0])], held, sem)
    fetch.start()
    nt, nv, nj = taken.shape[1:4]
    tiles = nj // 8
    weights = source_weights(me_ref[0], spectral_ref[...], nt)
    for k in range(peers):
        fetches[k].wait()
        for t in range(nt):
            m = k * nt + t
            for v in range(nv):
                x = taken[k, t, v].astype(jnp.float32)
                for b in range(tiles):
                    stage[b, m * 8 : (m + 1) * 8, v * LANES : (v + 1) * LANES] = x[b * 8 : (b + 1) * 8]
    for b in range(tiles):
        result[b] = jnp.dot(
            weights, stage[b].astype(jnp.bfloat16), preferred_element_type=jnp.float32
        )
    sent = []
    for k in range(peers):
        for t in range(nt):
            n = k * nt + t
            for v in range(nv):
                parts = [
                    result[b, n * 8 : (n + 1) * 8, v * LANES : (v + 1) * LANES] for b in range(tiles)
                ]
                made[k, t, v] = jnp.concatenate(parts, axis=0).astype(jnp.bfloat16)
        copy = pltpu.make_async_copy(made.at[k], outs[k], out_sems.at[k])
        copy.start()
        sent.append(copy)
    for copy in sent:
        copy.wait()
    fetch.wait()


def source_blocks(me, spectral, deriv_j, blocks):
    shape = blocks[0].shape
    nt, nv, nj, _ = shape
    peers = len(blocks)
    rows = peers * nt * 8
    vmem = pl.BlockSpec(memory_space=pltpu.VMEM)
    hbm = pl.BlockSpec(memory_space=pltpu.HBM)
    *sources, held = pl.pallas_call(
        source_kernel,
        out_shape=[pltpu.HBM(shape, jnp.bfloat16)] * peers
        + [pltpu.VMEM((deriv_j.shape[0] // 2, deriv_j.shape[1]), deriv_j.dtype)],
        in_specs=[pl.BlockSpec(memory_space=pltpu.SMEM), vmem, hbm] + [hbm] * peers,
        out_specs=[hbm] * peers + [vmem],
        scratch_shapes=[pltpu.VMEM((peers,) + shape, jnp.bfloat16)] * 2
        + [pltpu.VMEM((nj // 8, rows, nv * LANES), jnp.float32)] * 2
        + [pltpu.SemaphoreType.DMA((peers,))] * 2
        + [pltpu.SemaphoreType.DMA],
        compiler_params=pltpu.CompilerParams(vmem_limit_bytes=VMEM_LIMIT),
        cost_estimate=pl.CostEstimate(flops=420_000_000, bytes_accessed=10_000_000, transcendentals=0),
        name="source_blocks",
    )(me, spectral, in_hbm(deriv_j), *[in_hbm(b) for b in blocks])
    return sources, held


def local_kernel(
    state_ref, metric_i_ref, metric_j_ref, low_ref, high_ref, deriv_ref, out_ref, flux_ref
):
    nv, nj, ni = state_ref.shape[1:]
    metric_i = [metric_i_ref[c] for c in range(3)]
    cons = [state_ref[0, v].astype(jnp.float32) for v in range(nv)]
    inv, contra, pressure = primitives(cons, metric_i)
    for v, f in enumerate(flux_of(cons, metric_i, contra, pressure)):
        flux_ref[v * nj : (v + 1) * nj, :] = f
    radius_i = 0.25 * radius_of(metric_i, inv, contra, pressure)
    metric_j = [metric_j_ref[c] for c in range(3)]
    inv, contra, pressure = primitives(cons, metric_j)
    radius_j = 0.25 * radius_of(metric_j, inv, contra, pressure)
    term = lax.dot_general(
        flux_ref[...].astype(jnp.bfloat16),
        deriv_ref[...],
        (((1,), (1,)), ((), ())),
        preferred_element_type=jnp.float32,
    )
    row = lax.broadcasted_iota(jnp.int32, (nj, ni), 0)
    col = lax.broadcasted_iota(jnp.int32, (nj, ni), 1)
    low = low_ref[0].astype(jnp.float32)
    high = high_ref[0].astype(jnp.float32)
    for v in range(nv):
        c = cons[v]
        right = jnp.where(col == ni - 1, 0.0, pltpu.roll(c, ni - 1, 1))
        left = jnp.where(col == 0, 0.0, pltpu.roll(c, 1, 1))
        up = jnp.where(row == nj - 1, high[v : v + 1], pltpu.roll(c, nj - 1, 0))
        down = jnp.where(row == 0, low[v : v + 1], pltpu.roll(c, 1, 0))
        twice = 2.0 * c
        damping = radius_i * (right + left - twice) + radius_j * (up + down - twice)
        out_ref[0, v] = term[v * nj : (v + 1) * nj] - damping


def local_terms(state, metric_i, metric_j, low, high, deriv_i):
    nt, nv, nj, ni = state.shape
    whole3 = pl.BlockSpec((3, nj, ni), lambda t: (0, 0, 0))
    halo = pl.BlockSpec((1, nv, ni), lambda t: (t, 0, 0))
    per_t = pl.BlockSpec((1, nv, nj, ni), lambda t: (t, 0, 0, 0))
    return pl.pallas_call(
        local_kernel,
        grid=(nt,),
        out_shape=pltpu.HBM((nt, nv, nj, ni), jnp.float32),
        in_specs=[per_t, whole3, whole3, halo, halo, pl.BlockSpec((ni, ni), lambda t: (0, 0))],
        out_specs=per_t,
        scratch_shapes=[pltpu.VMEM((nv * nj, ni), jnp.float32)],
        compiler_params=pltpu.CompilerParams(vmem_limit_bytes=VMEM_LIMIT),
        cost_estimate=pl.CostEstimate(
            flops=2 * nt * nv * nj * ni * ni, bytes_accessed=11_000_000, transcendentals=600_000
        ),
        name="local_terms",
    )(*[in_hbm(x) for x in (state, metric_i, metric_j, low, high, deriv_i)])


def add_kernel(me_ref, partial_hbm, *refs):
    out_ref, partial_ref, taken, part_sems, in_sems = refs[-5:]
    sources = refs[:-5]
    nt, nv = out_ref.shape[:2]
    for t in range(nt):
        pltpu.make_async_copy(partial_hbm.at[t], partial_ref.at[t], part_sems.at[t]).start()
    for k, source in enumerate(sources):
        pltpu.make_async_copy(source, taken.at[k], in_sems.at[k]).start()
    for k, source in enumerate(sources):
        pltpu.make_async_copy(source, taken.at[k], in_sems.at[k]).wait()

    @pl.loop(0, nt)
    def _(t):
        pltpu.make_async_copy(partial_hbm.at[t], partial_ref.at[t], part_sems.at[t]).wait()
        for k in range(len(sources)):
            cols = pl.ds(pl.multiple_of((me_ref[0] ^ k) * LANES, LANES), LANES)
            for v in range(nv):
                out_ref[t, v, :, cols] = partial_ref[t, v, :, cols] + taken[k, t, v].astype(jnp.float32)


def add_sources(me, partial, sources):
    peers = len(sources)
    hbm = pl.BlockSpec(memory_space=pltpu.HBM)
    return pl.pallas_call(
        add_kernel,
        out_shape=pltpu.VMEM(partial.shape, jnp.float32),
        in_specs=[pl.BlockSpec(memory_space=pltpu.SMEM)] + [hbm] * (peers + 1),
        out_specs=pl.BlockSpec(memory_space=pltpu.VMEM),
        scratch_shapes=[
            pltpu.VMEM(partial.shape, jnp.float32),
            pltpu.VMEM((peers,) + sources[0].shape, jnp.bfloat16),
            pltpu.SemaphoreType.DMA((partial.shape[0],)),
            pltpu.SemaphoreType.DMA((peers,)),
        ],
        compiler_params=pltpu.CompilerParams(vmem_limit_bytes=VMEM_SMALL),
        cost_estimate=pl.CostEstimate(flops=1_000_000, bytes_accessed=8_000_000, transcendentals=0),
        name="add_sources",
    )(me, partial, *[in_hbm(x) for x in sources])


def slope_kernel(held_ref, lines_ref, deriv_hbm, out_hbm, rest_ref, out_ref, in_sem, sems):
    half = held_ref.shape[0]
    rest = pltpu.make_async_copy(deriv_hbm.at[pl.ds(half, half)], rest_ref, in_sem)
    rest.start()
    sizes = (256, 256, half - 512)

    def multiply(deriv_ref, base, first_sem):
        row = 0
        for c, size in enumerate(sizes):
            rows = pl.ds(base + row, size)
            out_ref[rows, :] = jnp.dot(
                deriv_ref[row : row + size, :], lines_ref[...], preferred_element_type=jnp.float32
            ).astype(jnp.bfloat16)
            sent = pltpu.make_async_copy(out_ref.at[rows], out_hbm.at[rows], sems.at[first_sem + c])
            sent.start()
            row += size

    @pl.loop(0, 3)
    def _(step):
        @pl.when(step == 0)
        def _():
            multiply(held_ref, 0, 0)

        @pl.when(step == 1)
        def _():
            rest.wait()
            multiply(rest_ref, half, len(sizes))

        @pl.when(step == 2)
        def _():
            row = 0
            for c, size in enumerate(sizes * 2):
                rows = pl.ds(row, size)
                pltpu.make_async_copy(out_ref.at[rows], out_hbm.at[rows], sems.at[c]).wait()
                row += size


def slope_lines(held, lines, deriv_j):
    size, width = lines.shape
    vmem = pl.BlockSpec(memory_space=pltpu.VMEM)
    hbm = pl.BlockSpec(memory_space=pltpu.HBM)
    return pl.pallas_call(
        slope_kernel,
        out_shape=pltpu.HBM((size, width), jnp.bfloat16),
        in_specs=[vmem, vmem, hbm],
        out_specs=hbm,
        scratch_shapes=[
            pltpu.VMEM(held.shape, jnp.bfloat16),
            pltpu.VMEM((size, width), jnp.bfloat16),
            pltpu.SemaphoreType.DMA,
            pltpu.SemaphoreType.DMA((6,)),
        ],
        compiler_params=pltpu.CompilerParams(vmem_limit_bytes=VMEM_SMALL),
        cost_estimate=pl.CostEstimate(
            flops=2 * size * size * width, bytes_accessed=7_000_000, transcendentals=0
        ),
        name="slope_lines",
    )(held, lines, in_hbm(deriv_j))


def finish_kernel(total_ref, slope_hbm, out_hbm, slope_ref, out_ref, in_sems, out_sems):
    nt, nv = total_ref.shape[:2]
    for t in range(nt):
        pltpu.make_async_copy(slope_hbm.at[t], slope_ref.at[t], in_sems.at[t]).start()

    @pl.loop(0, nt)
    def _(t):
        pltpu.make_async_copy(slope_hbm.at[t], slope_ref.at[t], in_sems.at[t]).wait()
        for b in range(slope_ref.shape[1]):
            cols = slice(b * LANES, (b + 1) * LANES)
            for v in range(nv):
                s = slope_ref[t, b, :, v * LANES : (v + 1) * LANES].astype(jnp.float32)
                out_ref[t, v, :, cols] = (total_ref[t, v, :, cols] + s).astype(jnp.bfloat16)
        pltpu.make_async_copy(out_ref.at[t], out_hbm.at[t], out_sems.at[t]).start()

    @pl.loop(0, nt)
    def _(t):
        pltpu.make_async_copy(out_ref.at[t], out_hbm.at[t], out_sems.at[t]).wait()


def finish(total, slope):
    nt = total.shape[0]
    hbm = pl.BlockSpec(memory_space=pltpu.HBM)
    return pl.pallas_call(
        finish_kernel,
        out_shape=jax.ShapeDtypeStruct(total.shape, jnp.bfloat16),
        in_specs=[pl.BlockSpec(memory_space=pltpu.VMEM), hbm],
        out_specs=hbm,
        scratch_shapes=[
            pltpu.VMEM(slope.shape, jnp.bfloat16),
            pltpu.VMEM(total.shape, jnp.bfloat16),
            pltpu.SemaphoreType.DMA((nt,)),
            pltpu.SemaphoreType.DMA((nt,)),
        ],
        compiler_params=pltpu.CompilerParams(vmem_limit_bytes=VMEM_LIMIT),
        cost_estimate=pl.CostEstimate(flops=1_000_000, bytes_accessed=7_000_000, transcendentals=0),
        name="finish",
    )(total, in_hbm(slope))


def on_device(state, spectral, deriv_i, deriv_j, metric_i, metric_j):
    nt, nv, nj, ni = state.shape
    count = lax.axis_size("space")
    forward = [(i, i + 1) for i in range(count - 1)]
    backward = [(target, source) for source, target in forward]
    peers = lax.axis_size("tm")
    swaps = [[(i, i ^ k) for i in range(peers)] for k in range(peers)]
    rank = lax.axis_index("tm")
    me = jnp.reshape(rank, (1,)).astype(jnp.int32)
    outgoing = flux_j_blocks(state, metric_j).reshape(count, nj, nv * LANES)
    lines = lax.all_to_all(outgoing, "space", split_axis=0, concat_axis=0, tiled=True)
    first, last, own = pack_blocks(me, state)
    low = lax.ppermute(last, "space", forward)
    high = lax.ppermute(first, "space", backward)
    blocks = own[:1] + [lax.ppermute(own[k], "tm", swaps[k]) for k in range(1, peers)]
    sources, held = source_blocks(me, spectral, deriv_j, blocks)
    sources = sources[:1] + [lax.ppermute(sources[k], "tm", swaps[k]) for k in range(1, peers)]
    slope = slope_lines(held, lines.reshape(count * nj, nv * LANES), deriv_j)
    slope, low, high = lax.optimization_barrier((slope, low, high))
    slope = lax.all_to_all(
        slope.reshape(count, nj, nv * LANES), "space", split_axis=0, concat_axis=0, tiled=True
    )
    partial = local_terms(state, metric_i, metric_j, low, high, deriv_i)
    total = add_sources(me, partial, sources)
    return finish(total, slope.reshape(nt, ni // LANES, nj, nv * LANES))


def solution(mesh):
    return jax.shard_map(
        on_device,
        mesh=mesh,
        in_specs=(
            P("tm", None, "space", None),
            P(),
            P(),
            P(),
            P(None, "space", None),
            P(None, "space", None),
        ),
        out_specs=P("tm", None, "space", None),
        check_vma=False,
    )
```

```python
import jax
import jax.numpy as jnp
from jax import lax
from jax.experimental import pallas as pl
from jax.experimental.pallas import tpu as pltpu
from jax.sharding import PartitionSpec as P

LANES = 128
VMEM_LIMIT = 28 * 1024 * 1024
VMEM_SMALL = 12 * 1024 * 1024


def primitives(cons, metric):
    rho, mx, my, mz, energy = cons
    ax, ay, az = metric
    inv = 1.0 / rho
    contra = (ax * mx + ay * my + az * mz) * inv
    pressure = 0.4 * (energy - 0.5 * (mx * mx + my * my + mz * mz) * inv)
    return inv, contra, pressure


def flux_of(cons, metric, contra, pressure):
    rho, mx, my, mz, energy = cons
    ax, ay, az = metric
    return (
        rho * contra,
        mx * contra + ax * pressure,
        my * contra + ay * pressure,
        mz * contra + az * pressure,
        (energy + pressure) * contra,
    )


def radius_of(metric, inv, contra, pressure):
    ax, ay, az = metric
    return jnp.abs(contra) + jnp.sqrt(1.4 * pressure * inv * (ax * ax + ay * ay + az * az))


def flux_j_kernel(state_hbm, metric_hbm, out_hbm, state_ref, metric_ref, out_ref, in_sems, out_sems):
    nt = state_ref.shape[0]
    blocks = out_ref.shape[1]
    metric_copy = pltpu.make_async_copy(metric_hbm, metric_ref, in_sems.at[nt])
    metric_copy.start()
    copies = [
        pltpu.make_async_copy(state_hbm.at[t], state_ref.at[t], in_sems.at[t]) for t in range(nt)
    ]
    for copy in copies:
        copy.start()
    metric_copy.wait()

    @pl.loop(0, nt)
    def _(t):
        pltpu.make_async_copy(state_hbm.at[t], state_ref.at[t], in_sems.at[t]).wait()
        for b in range(blocks):
            cols = slice(b * LANES, (b + 1) * LANES)
            cons = [state_ref[t, v, :, cols].astype(jnp.float32) for v in range(5)]
            metric = [metric_ref[c, :, cols] for c in range(3)]
            _, contra, pressure = primitives(cons, metric)
            for v, f in enumerate(flux_of(cons, metric, contra, pressure)):
                out_ref[t, b, :, v * LANES : (v + 1) * LANES] = f.astype(jnp.bfloat16)
        pltpu.make_async_copy(out_ref.at[t], out_hbm.at[t], out_sems.at[t]).start()

    @pl.loop(0, nt)
    def _(t):
        pltpu.make_async_copy(out_ref.at[t], out_hbm.at[t], out_sems.at[t]).wait()


def in_hbm(x):
    return pltpu.with_memory_space_constraint(x, pltpu.HBM)


def flux_j_blocks(state, metric_j):
    nt, nv, nj, ni = state.shape
    blocks = ni // LANES
    hbm = pl.BlockSpec(memory_space=pltpu.HBM)
    shape = (nt, blocks, nj, nv * LANES)
    return pl.pallas_call(
        flux_j_kernel,
        out_shape=pltpu.HBM(shape, jnp.bfloat16),
        in_specs=[hbm, hbm],
        out_specs=hbm,
        scratch_shapes=[
            pltpu.VMEM(state.shape, jnp.bfloat16),
            pltpu.VMEM(metric_j.shape, jnp.float32),
            pltpu.VMEM(shape, jnp.bfloat16),
            pltpu.SemaphoreType.DMA((nt + 1,)),
            pltpu.SemaphoreType.DMA((nt,)),
        ],
        compiler_params=pltpu.CompilerParams(vmem_limit_bytes=VMEM_LIMIT),
        cost_estimate=pl.CostEstimate(flops=10_000_000, bytes_accessed=4_000_000, transcendentals=200_000),
        name="flux_j",
    )(in_hbm(state), in_hbm(metric_j))


def pack_kernel(me_ref, state_ref, first_ref, last_ref, *outs):
    nv, nj = state_ref.shape[1:3]
    for k, out in enumerate(outs):
        cols = pl.ds(pl.multiple_of((me_ref[0] ^ k) * LANES, LANES), LANES)
        for v in range(nv):
            out[0, v] = state_ref[0, v, :, cols]
    cons = [state_ref[0, v].astype(jnp.float32) for v in range(nv)]
    first_ref[0] = jnp.concatenate([c[:1] for c in cons], axis=0).astype(jnp.bfloat16)
    last_ref[0] = jnp.concatenate([c[nj - 1 :] for c in cons], axis=0).astype(jnp.bfloat16)


def pack_blocks(me, state):
    nt, nv, nj, ni = state.shape
    peers = ni // LANES
    block = pl.BlockSpec((1, nv, nj, LANES), lambda t: (t, 0, 0, 0))
    edge = pl.BlockSpec((1, nv, ni), lambda t: (t, 0, 0))
    first, last, *blocks = pl.pallas_call(
        pack_kernel,
        grid=(nt,),
        out_shape=[pltpu.HBM((nt, nv, ni), state.dtype)] * 2
        + [pltpu.HBM((nt, nv, nj, LANES), state.dtype)] * peers,
        in_specs=[
            pl.BlockSpec(memory_space=pltpu.SMEM),
            pl.BlockSpec((1, nv, nj, ni), lambda t: (t, 0, 0, 0)),
        ],
        out_specs=[edge] * 2 + [block] * peers,
        compiler_params=pltpu.CompilerParams(vmem_limit_bytes=VMEM_LIMIT),
        cost_estimate=pl.CostEstimate(flops=0, bytes_accessed=3_300_000, transcendentals=0),
        name="pack_blocks",
    )(me, in_hbm(state))
    return first, last, blocks


def source_weights(me, spectral, nt):
    size = spectral.shape[0]
    row = lax.broadcasted_iota(jnp.int32, (size * 8, size), 0)
    col = lax.broadcasted_iota(jnp.int32, (size * 8, size), 1)
    instance = (me ^ (row // (nt * 8))) * nt + (row // 8) % nt
    pick = jnp.where(instance == col, 1.0, 0.0).astype(jnp.bfloat16)
    rows = jnp.dot(pick, spectral, preferred_element_type=jnp.float32).astype(jnp.bfloat16)
    full = lax.dot_general(
        rows, pick, (((1,), (1,)), ((), ())), preferred_element_type=jnp.float32
    )
    r = lax.broadcasted_iota(jnp.int32, full.shape, 0)
    c = lax.broadcasted_iota(jnp.int32, full.shape, 1)
    return jnp.where(r % 8 == c % 8, full, 0.0).astype(jnp.bfloat16)


def source_kernel(me_ref, spectral_ref, deriv_hbm, *refs):
    taken, made, stage, result, in_sems, out_sems, sem = refs[-7:]
    peers = taken.shape[0]
    ins, outs, held = refs[:peers], refs[peers : 2 * peers], refs[2 * peers]
    fetches = [pltpu.make_async_copy(ins[k], taken.at[k], in_sems.at[k]) for k in range(peers)]
    for copy in fetches:
        copy.start()
    fetch = pltpu.make_async_copy(deriv_hbm.at[pl.ds(0, held.shape[0])], held, sem)
    fetch.start()
    nt, nv, nj = taken.shape[1:4]
    tiles = nj // 8
    weights = source_weights(me_ref[0], spectral_ref[...], nt)
    for k in range(peers):
        fetches[k].wait()
        for t in range(nt):
            m = k * nt + t
            for v in range(nv):
                x = taken[k, t, v].astype(jnp.float32)
                for b in range(tiles):
                    stage[b, m * 8 : (m + 1) * 8, v * LANES : (v + 1) * LANES] = x[b * 8 : (b + 1) * 8]
    for b in range(tiles):
        result[b] = jnp.dot(
            weights, stage[b].astype(jnp.bfloat16), preferred_element_type=jnp.float32
        )
    sent = []
    for k in range(peers):
        for t in range(nt):
            n = k * nt + t
            for v in range(nv):
                parts = [
                    result[b, n * 8 : (n + 1) * 8, v * LANES : (v + 1) * LANES] for b in range(tiles)
                ]
                made[k, t, v] = jnp.concatenate(parts, axis=0).astype(jnp.bfloat16)
        copy = pltpu.make_async_copy(made.at[k], outs[k], out_sems.at[k])
        copy.start()
        sent.append(copy)
    for copy in sent:
        copy.wait()
    fetch.wait()


def source_blocks(me, spectral, deriv_j, blocks):
    shape = blocks[0].shape
    nt, nv, nj, _ = shape
    peers = len(blocks)
    rows = peers * nt * 8
    vmem = pl.BlockSpec(memory_space=pltpu.VMEM)
    hbm = pl.BlockSpec(memory_space=pltpu.HBM)
    *sources, held = pl.pallas_call(
        source_kernel,
        out_shape=[pltpu.HBM(shape, jnp.bfloat16)] * peers
        + [pltpu.VMEM((deriv_j.shape[0] // 2, deriv_j.shape[1]), deriv_j.dtype)],
        in_specs=[pl.BlockSpec(memory_space=pltpu.SMEM), vmem, hbm] + [hbm] * peers,
        out_specs=[hbm] * peers + [vmem],
        scratch_shapes=[pltpu.VMEM((peers,) + shape, jnp.bfloat16)] * 2
        + [pltpu.VMEM((nj // 8, rows, nv * LANES), jnp.float32)] * 2
        + [pltpu.SemaphoreType.DMA((peers,))] * 2
        + [pltpu.SemaphoreType.DMA],
        compiler_params=pltpu.CompilerParams(vmem_limit_bytes=VMEM_LIMIT),
        cost_estimate=pl.CostEstimate(flops=420_000_000, bytes_accessed=10_000_000, transcendentals=0),
        name="source_blocks",
    )(me, spectral, in_hbm(deriv_j), *[in_hbm(b) for b in blocks])
    return sources, held


def local_kernel(
    state_ref, metric_i_ref, metric_j_ref, low_ref, high_ref, deriv_ref, out_ref, flux_ref
):
    nv, nj, ni = state_ref.shape[1:]
    metric_i = [metric_i_ref[c] for c in range(3)]
    cons = [state_ref[0, v].astype(jnp.float32) for v in range(nv)]
    inv, contra, pressure = primitives(cons, metric_i)
    for v, f in enumerate(flux_of(cons, metric_i, contra, pressure)):
        flux_ref[v * nj : (v + 1) * nj, :] = f
    radius_i = 0.25 * radius_of(metric_i, inv, contra, pressure)
    metric_j = [metric_j_ref[c] for c in range(3)]
    inv, contra, pressure = primitives(cons, metric_j)
    radius_j = 0.25 * radius_of(metric_j, inv, contra, pressure)
    term = lax.dot_general(
        flux_ref[...].astype(jnp.bfloat16),
        deriv_ref[...],
        (((1,), (1,)), ((), ())),
        preferred_element_type=jnp.float32,
    )
    row = lax.broadcasted_iota(jnp.int32, (nj, ni), 0)
    col = lax.broadcasted_iota(jnp.int32, (nj, ni), 1)
    low = low_ref[0].astype(jnp.float32)
    high = high_ref[0].astype(jnp.float32)
    for v in range(nv):
        c = cons[v]
        right = jnp.where(col == ni - 1, 0.0, pltpu.roll(c, ni - 1, 1))
        left = jnp.where(col == 0, 0.0, pltpu.roll(c, 1, 1))
        up = jnp.where(row == nj - 1, high[v : v + 1], pltpu.roll(c, nj - 1, 0))
        down = jnp.where(row == 0, low[v : v + 1], pltpu.roll(c, 1, 0))
        twice = 2.0 * c
        damping = radius_i * (right + left - twice) + radius_j * (up + down - twice)
        out_ref[0, v] = term[v * nj : (v + 1) * nj] - damping


def local_terms(state, metric_i, metric_j, low, high, deriv_i):
    nt, nv, nj, ni = state.shape
    whole3 = pl.BlockSpec((3, nj, ni), lambda t: (0, 0, 0))
    halo = pl.BlockSpec((1, nv, ni), lambda t: (t, 0, 0))
    per_t = pl.BlockSpec((1, nv, nj, ni), lambda t: (t, 0, 0, 0))
    return pl.pallas_call(
        local_kernel,
        grid=(nt,),
        out_shape=pltpu.HBM((nt, nv, nj, ni), jnp.float32),
        in_specs=[per_t, whole3, whole3, halo, halo, pl.BlockSpec((ni, ni), lambda t: (0, 0))],
        out_specs=per_t,
        scratch_shapes=[pltpu.VMEM((nv * nj, ni), jnp.float32)],
        compiler_params=pltpu.CompilerParams(vmem_limit_bytes=VMEM_LIMIT),
        cost_estimate=pl.CostEstimate(
            flops=2 * nt * nv * nj * ni * ni, bytes_accessed=11_000_000, transcendentals=600_000
        ),
        name="local_terms",
    )(in_hbm(state), in_hbm(metric_i), in_hbm(metric_j), low, high, in_hbm(deriv_i))


def add_kernel(me_ref, partial_hbm, *refs):
    out_ref, partial_ref, taken, part_sems, in_sems = refs[-5:]
    sources = refs[:-5]
    nt, nv = out_ref.shape[:2]
    for t in range(nt):
        pltpu.make_async_copy(partial_hbm.at[t], partial_ref.at[t], part_sems.at[t]).start()
    for k, source in enumerate(sources):
        pltpu.make_async_copy(source, taken.at[k], in_sems.at[k]).start()
    for k, source in enumerate(sources):
        pltpu.make_async_copy(source, taken.at[k], in_sems.at[k]).wait()

    @pl.loop(0, nt)
    def _(t):
        pltpu.make_async_copy(partial_hbm.at[t], partial_ref.at[t], part_sems.at[t]).wait()
        for k in range(len(sources)):
            cols = pl.ds(pl.multiple_of((me_ref[0] ^ k) * LANES, LANES), LANES)
            for v in range(nv):
                total = partial_ref[t, v, :, cols] + taken[k, t, v].astype(jnp.float32)
                out_ref[t, v, :, cols] = total.astype(jnp.bfloat16)


def add_sources(me, partial, sources):
    peers = len(sources)
    hbm = pl.BlockSpec(memory_space=pltpu.HBM)
    return pl.pallas_call(
        add_kernel,
        out_shape=pltpu.VMEM(partial.shape, jnp.bfloat16),
        in_specs=[pl.BlockSpec(memory_space=pltpu.SMEM)] + [hbm] * (peers + 1),
        out_specs=pl.BlockSpec(memory_space=pltpu.VMEM),
        scratch_shapes=[
            pltpu.VMEM(partial.shape, jnp.float32),
            pltpu.VMEM((peers,) + sources[0].shape, jnp.bfloat16),
            pltpu.SemaphoreType.DMA((partial.shape[0],)),
            pltpu.SemaphoreType.DMA((peers,)),
        ],
        compiler_params=pltpu.CompilerParams(vmem_limit_bytes=VMEM_SMALL),
        cost_estimate=pl.CostEstimate(flops=1_000_000, bytes_accessed=8_000_000, transcendentals=0),
        name="add_sources",
    )(me, partial, *[in_hbm(x) for x in sources])


def slope_kernel(held_ref, lines_ref, deriv_hbm, out_hbm, rest_ref, out_ref, in_sem, sems):
    half = held_ref.shape[0]
    rest = pltpu.make_async_copy(deriv_hbm.at[pl.ds(half, half)], rest_ref, in_sem)
    rest.start()
    sizes = (256, 256, half - 512)

    def multiply(deriv_ref, base, first_sem):
        row = 0
        for c, size in enumerate(sizes):
            rows = pl.ds(base + row, size)
            out_ref[rows, :] = jnp.dot(
                deriv_ref[row : row + size, :], lines_ref[...], preferred_element_type=jnp.float32
            ).astype(jnp.bfloat16)
            sent = pltpu.make_async_copy(out_ref.at[rows], out_hbm.at[rows], sems.at[first_sem + c])
            sent.start()
            row += size

    @pl.loop(0, 3)
    def _(step):
        @pl.when(step == 0)
        def _():
            multiply(held_ref, 0, 0)

        @pl.when(step == 1)
        def _():
            rest.wait()
            multiply(rest_ref, half, len(sizes))

        @pl.when(step == 2)
        def _():
            row = 0
            for c, size in enumerate(sizes * 2):
                rows = pl.ds(row, size)
                pltpu.make_async_copy(out_ref.at[rows], out_hbm.at[rows], sems.at[c]).wait()
                row += size


def slope_lines(held, lines, deriv_j):
    size, width = lines.shape
    vmem = pl.BlockSpec(memory_space=pltpu.VMEM)
    hbm = pl.BlockSpec(memory_space=pltpu.HBM)
    return pl.pallas_call(
        slope_kernel,
        out_shape=pltpu.HBM((size, width), jnp.bfloat16),
        in_specs=[vmem, vmem, hbm],
        out_specs=hbm,
        scratch_shapes=[
            pltpu.VMEM(held.shape, jnp.bfloat16),
            pltpu.VMEM((size, width), jnp.bfloat16),
            pltpu.SemaphoreType.DMA,
            pltpu.SemaphoreType.DMA((6,)),
        ],
        compiler_params=pltpu.CompilerParams(vmem_limit_bytes=VMEM_SMALL),
        cost_estimate=pl.CostEstimate(
            flops=2 * size * size * width, bytes_accessed=7_000_000, transcendentals=0
        ),
        name="slope_lines",
    )(held, lines, in_hbm(deriv_j))


def finish_kernel(total_ref, slope_ref, out_hbm, out_ref, sems):
    nt, nv = total_ref.shape[:2]

    @pl.loop(0, nt)
    def _(t):
        for b in range(slope_ref.shape[1]):
            cols = slice(b * LANES, (b + 1) * LANES)
            for v in range(nv):
                s = slope_ref[t, b, :, v * LANES : (v + 1) * LANES].astype(jnp.float32)
                total = total_ref[t, v, :, cols].astype(jnp.float32)
                out_ref[t, v, :, cols] = (total + s).astype(jnp.bfloat16)
        pltpu.make_async_copy(out_ref.at[t], out_hbm.at[t], sems.at[t]).start()

    @pl.loop(0, nt)
    def _(t):
        pltpu.make_async_copy(out_ref.at[t], out_hbm.at[t], sems.at[t]).wait()


def finish(total, slope):
    nt = total.shape[0]
    vmem = pl.BlockSpec(memory_space=pltpu.VMEM)
    return pl.pallas_call(
        finish_kernel,
        out_shape=jax.ShapeDtypeStruct(total.shape, jnp.bfloat16),
        in_specs=[vmem, vmem],
        out_specs=pl.BlockSpec(memory_space=pltpu.HBM),
        scratch_shapes=[
            pltpu.VMEM(total.shape, jnp.bfloat16),
            pltpu.SemaphoreType.DMA((nt,)),
        ],
        compiler_params=pltpu.CompilerParams(vmem_limit_bytes=VMEM_SMALL),
        cost_estimate=pl.CostEstimate(flops=1_000_000, bytes_accessed=5_000_000, transcendentals=0),
        name="finish",
    )(total, slope)


def on_device(state, spectral, deriv_i, deriv_j, metric_i, metric_j):
    nt, nv, nj, ni = state.shape
    count = lax.axis_size("space")
    forward = [(i, i + 1) for i in range(count - 1)]
    backward = [(target, source) for source, target in forward]
    peers = lax.axis_size("tm")
    swaps = [[(i, i ^ k) for i in range(peers)] for k in range(peers)]
    rank = lax.axis_index("tm")
    me = jnp.reshape(rank, (1,)).astype(jnp.int32)
    outgoing = flux_j_blocks(state, metric_j).reshape(count, nj, nv * LANES)
    lines = lax.all_to_all(outgoing, "space", split_axis=0, concat_axis=0, tiled=True)
    first, last, own = pack_blocks(me, state)
    low = lax.ppermute(last, "space", forward)
    high = lax.ppermute(first, "space", backward)
    blocks = own[:1] + [lax.ppermute(own[k], "tm", swaps[k]) for k in range(1, peers)]
    sources, held = source_blocks(me, spectral, deriv_j, blocks)
    sources = sources[:1] + [lax.ppermute(sources[k], "tm", swaps[k]) for k in range(1, peers)]
    slope = slope_lines(held, lines.reshape(count * nj, nv * LANES), deriv_j)
    slope, low, high = lax.optimization_barrier((slope, low, high))
    slope = lax.all_to_all(
        slope.reshape(count, nj, nv * LANES), "space", split_axis=0, concat_axis=0, tiled=True
    )
    partial = local_terms(state, metric_i, metric_j, low, high, deriv_i)
    total = add_sources(me, partial, sources)
    return finish(total, slope.reshape(nt, ni // LANES, nj, nv * LANES))


def solution(mesh):
    return jax.shard_map(
        on_device,
        mesh=mesh,
        in_specs=(
            P("tm", None, "space", None),
            P(),
            P(),
            P(),
            P(None, "space", None),
            P(None, "space", None),
        ),
        out_specs=P("tm", None, "space", None),
        check_vma=False,
    )
```

```python
import functools

import jax
import jax.numpy as jnp
from jax import lax
from jax.experimental import pallas as pl
from jax.experimental.pallas import tpu as pltpu
from jax.sharding import PartitionSpec as P

LANES = 128
ORDER = (16, 25, 18, 31, 29, 20, 0, 4, 10, 7, 14, 17, 22, 28, 15, 12, 13, 27, 1, 24, 6, 19, 8, 9, 21, 23, 5, 26, 11, 30, 2, 3)
VMEM_LIMIT = 28 * 1024 * 1024
VMEM_SMALL = 12 * 1024 * 1024


def primitives(cons, metric):
    rho, mx, my, mz, energy = cons
    ax, ay, az = metric
    inv = 1.0 / rho
    contra = (ax * mx + ay * my + az * mz) * inv
    pressure = 0.4 * (energy - 0.5 * (mx * mx + my * my + mz * mz) * inv)
    return inv, contra, pressure


def flux_of(cons, metric, contra, pressure):
    rho, mx, my, mz, energy = cons
    ax, ay, az = metric
    return (
        rho * contra,
        mx * contra + ax * pressure,
        my * contra + ay * pressure,
        mz * contra + az * pressure,
        (energy + pressure) * contra,
    )


def radius_of(metric, inv, contra, pressure):
    ax, ay, az = metric
    return jnp.abs(contra) + jnp.sqrt(1.4 * pressure * inv * (ax * ax + ay * ay + az * az))


def flux_j_kernel(state_hbm, metric_hbm, out_hbm, state_ref, metric_ref, out_ref, in_sems, out_sems):
    nt = state_ref.shape[0]
    blocks = out_ref.shape[1]
    metric_copy = pltpu.make_async_copy(metric_hbm, metric_ref, in_sems.at[nt])
    metric_copy.start()
    copies = [
        pltpu.make_async_copy(state_hbm.at[t], state_ref.at[t], in_sems.at[t]) for t in range(nt)
    ]
    for copy in copies:
        copy.start()
    metric_copy.wait()

    @pl.loop(0, nt)
    def _(t):
        pltpu.make_async_copy(state_hbm.at[t], state_ref.at[t], in_sems.at[t]).wait()
        for b in range(blocks):
            cols = slice(b * LANES, (b + 1) * LANES)
            cons = [state_ref[t, v, :, cols].astype(jnp.float32) for v in range(5)]
            metric = [metric_ref[c, :, cols] for c in range(3)]
            _, contra, pressure = primitives(cons, metric)
            for v, f in enumerate(flux_of(cons, metric, contra, pressure)):
                out_ref[t, b, :, v * LANES : (v + 1) * LANES] = f.astype(jnp.bfloat16)
        pltpu.make_async_copy(out_ref.at[t], out_hbm.at[t], out_sems.at[t]).start()

    @pl.loop(0, nt)
    def _(t):
        pltpu.make_async_copy(out_ref.at[t], out_hbm.at[t], out_sems.at[t]).wait()


def in_hbm(x):
    return pltpu.with_memory_space_constraint(x, pltpu.HBM)


def flux_j_blocks(state, metric_j):
    nt, nv, nj, ni = state.shape
    blocks = ni // LANES
    hbm = pl.BlockSpec(memory_space=pltpu.HBM)
    shape = (nt, blocks, nj, nv * LANES)
    return pl.pallas_call(
        flux_j_kernel,
        out_shape=pltpu.HBM(shape, jnp.bfloat16),
        in_specs=[hbm, hbm],
        out_specs=hbm,
        scratch_shapes=[
            pltpu.VMEM(state.shape, jnp.bfloat16),
            pltpu.VMEM(metric_j.shape, jnp.float32),
            pltpu.VMEM(shape, jnp.bfloat16),
            pltpu.SemaphoreType.DMA((nt + 1,)),
            pltpu.SemaphoreType.DMA((nt,)),
        ],
        compiler_params=pltpu.CompilerParams(vmem_limit_bytes=VMEM_LIMIT),
        cost_estimate=pl.CostEstimate(flops=10_000_000, bytes_accessed=4_000_000, transcendentals=200_000),
        name="flux_j",
    )(in_hbm(state), in_hbm(metric_j))


def pack_kernel(me_ref, state_hbm, *refs):
    state_ref, out_ref, edge_ref, in_sems, out_sems, edge_sems = refs[-6:]
    edges, outs = refs[:2], refs[2:-6]
    nt, nv, nj = state_ref.shape[:3]
    for t in range(nt):
        pltpu.make_async_copy(state_hbm.at[t], state_ref.at[t], in_sems.at[t]).start()

    @pl.loop(0, nt)
    def _(t):
        pltpu.make_async_copy(state_hbm.at[t], state_ref.at[t], in_sems.at[t]).wait()
        for k, out in enumerate(outs):
            cols = pl.ds(pl.multiple_of((me_ref[0] ^ k) * LANES, LANES), LANES)
            for v in range(nv):
                out_ref[k, t, v] = state_ref[t, v, :, cols]
            pltpu.make_async_copy(out_ref.at[k, t], out.at[t], out_sems.at[k, t]).start()
        cons = [state_ref[t, v].astype(jnp.float32) for v in range(nv)]
        for e, row in enumerate((0, nj - 1)):
            rows = jnp.concatenate([c[row : row + 1] for c in cons], axis=0)
            edge_ref[e, t] = rows.astype(jnp.bfloat16)
            pltpu.make_async_copy(edge_ref.at[e, t], edges[e].at[t], edge_sems.at[e, t]).start()

    @pl.loop(0, nt)
    def _(t):
        for k, out in enumerate(outs):
            pltpu.make_async_copy(out_ref.at[k, t], out.at[t], out_sems.at[k, t]).wait()
        for e, edge in enumerate(edges):
            pltpu.make_async_copy(edge_ref.at[e, t], edge.at[t], edge_sems.at[e, t]).wait()


def pack_blocks(me, state):
    nt, nv, nj, ni = state.shape
    peers = ni // LANES
    hbm = pl.BlockSpec(memory_space=pltpu.HBM)
    block = (nt, nv, nj, LANES)
    edge = (nt, nv, ni)
    first, last, *blocks = pl.pallas_call(
        pack_kernel,
        out_shape=[pltpu.HBM(edge, state.dtype)] * 2 + [pltpu.HBM(block, state.dtype)] * peers,
        in_specs=[pl.BlockSpec(memory_space=pltpu.SMEM), hbm],
        out_specs=[hbm] * (peers + 2),
        scratch_shapes=[
            pltpu.VMEM(state.shape, state.dtype),
            pltpu.VMEM((peers,) + block, state.dtype),
            pltpu.VMEM((2,) + edge, state.dtype),
            pltpu.SemaphoreType.DMA((nt,)),
            pltpu.SemaphoreType.DMA((peers, nt)),
            pltpu.SemaphoreType.DMA((2, nt)),
        ],
        compiler_params=pltpu.CompilerParams(vmem_limit_bytes=VMEM_SMALL),
        cost_estimate=pl.CostEstimate(flops=0, bytes_accessed=3_300_000, transcendentals=0),
        name="pack_blocks",
    )(me, in_hbm(state))
    return first, last, blocks


def source_weights(me, spectral, nt):
    size = spectral.shape[0]
    row = lax.broadcasted_iota(jnp.int32, (size * 8, size), 0)
    col = lax.broadcasted_iota(jnp.int32, (size * 8, size), 1)
    instance = (me ^ (row // (nt * 8))) * nt + (row // 8) % nt
    pick = jnp.where(instance == col, 1.0, 0.0).astype(jnp.bfloat16)
    rows = jnp.dot(pick, spectral, preferred_element_type=jnp.float32).astype(jnp.bfloat16)
    full = lax.dot_general(
        rows, pick, (((1,), (1,)), ((), ())), preferred_element_type=jnp.float32
    )
    r = lax.broadcasted_iota(jnp.int32, full.shape, 0)
    c = lax.broadcasted_iota(jnp.int32, full.shape, 1)
    return jnp.where(r % 8 == c % 8, full, 0.0).astype(jnp.bfloat16)


def source_kernel(me_ref, spectral_ref, deriv_hbm, *refs):
    taken, made, stage, result, in_sems, out_sems, sem = refs[-7:]
    peers = taken.shape[0]
    ins, outs, held = refs[:peers], refs[peers : 2 * peers], refs[2 * peers]
    fetches = [pltpu.make_async_copy(ins[k], taken.at[k], in_sems.at[k]) for k in range(peers)]
    for copy in fetches:
        copy.start()
    fetch = pltpu.make_async_copy(deriv_hbm.at[pl.ds(0, held.shape[0])], held, sem)
    fetch.start()
    nt, nv, nj = taken.shape[1:4]
    tiles = nj // 8
    weights = source_weights(me_ref[0], spectral_ref[...], nt)
    for k in range(peers):
        fetches[k].wait()
        for t in range(nt):
            m = k * nt + t
            for v in range(nv):
                x = taken[k, t, v].astype(jnp.float32)
                for b in range(tiles):
                    stage[b, m * 8 : (m + 1) * 8, v * LANES : (v + 1) * LANES] = x[b * 8 : (b + 1) * 8]
    for b in range(tiles):
        result[b] = jnp.dot(
            weights, stage[b].astype(jnp.bfloat16), preferred_element_type=jnp.float32
        )
    sent = []
    for k in range(peers):
        for t in range(nt):
            n = k * nt + t
            for v in range(nv):
                parts = [
                    result[b, n * 8 : (n + 1) * 8, v * LANES : (v + 1) * LANES] for b in range(tiles)
                ]
                made[k, t, v] = jnp.concatenate(parts, axis=0).astype(jnp.bfloat16)
        copy = pltpu.make_async_copy(made.at[k], outs[k], out_sems.at[k])
        copy.start()
        sent.append(copy)
    for copy in sent:
        copy.wait()
    fetch.wait()


def source_blocks(me, spectral, deriv_j, blocks):
    shape = blocks[0].shape
    nt, nv, nj, _ = shape
    peers = len(blocks)
    rows = peers * nt * 8
    vmem = pl.BlockSpec(memory_space=pltpu.VMEM)
    hbm = pl.BlockSpec(memory_space=pltpu.HBM)
    *sources, held = pl.pallas_call(
        source_kernel,
        out_shape=[pltpu.HBM(shape, jnp.bfloat16)] * peers
        + [pltpu.VMEM((deriv_j.shape[0] // 2, deriv_j.shape[1]), deriv_j.dtype)],
        in_specs=[pl.BlockSpec(memory_space=pltpu.SMEM), vmem, hbm] + [hbm] * peers,
        out_specs=[hbm] * peers + [vmem],
        scratch_shapes=[pltpu.VMEM((peers,) + shape, jnp.bfloat16)] * 2
        + [pltpu.VMEM((nj // 8, rows, nv * LANES), jnp.float32)] * 2
        + [pltpu.SemaphoreType.DMA((peers,))] * 2
        + [pltpu.SemaphoreType.DMA],
        compiler_params=pltpu.CompilerParams(vmem_limit_bytes=VMEM_LIMIT),
        cost_estimate=pl.CostEstimate(flops=420_000_000, bytes_accessed=10_000_000, transcendentals=0),
        name="source_blocks",
    )(me, spectral, in_hbm(deriv_j), *[in_hbm(b) for b in blocks])
    return sources, held


def local_kernel(
    state_ref, metric_i_ref, metric_j_ref, low_ref, high_ref, deriv_ref, out_ref, flux_ref
):
    nv, nj, ni = state_ref.shape[1:]
    metric_i = [metric_i_ref[c] for c in range(3)]
    cons = [state_ref[0, v].astype(jnp.float32) for v in range(nv)]
    inv, contra, pressure = primitives(cons, metric_i)
    for v, f in enumerate(flux_of(cons, metric_i, contra, pressure)):
        flux_ref[v * nj : (v + 1) * nj, :] = f
    radius_i = 0.25 * radius_of(metric_i, inv, contra, pressure)
    metric_j = [metric_j_ref[c] for c in range(3)]
    inv, contra, pressure = primitives(cons, metric_j)
    radius_j = 0.25 * radius_of(metric_j, inv, contra, pressure)
    term = lax.dot_general(
        flux_ref[...].astype(jnp.bfloat16),
        deriv_ref[...],
        (((1,), (1,)), ((), ())),
        preferred_element_type=jnp.float32,
    )
    row = lax.broadcasted_iota(jnp.int32, (nj, ni), 0)
    col = lax.broadcasted_iota(jnp.int32, (nj, ni), 1)
    low = low_ref[0].astype(jnp.float32)
    high = high_ref[0].astype(jnp.float32)
    for v in range(nv):
        c = cons[v]
        right = jnp.where(col == ni - 1, 0.0, pltpu.roll(c, ni - 1, 1))
        left = jnp.where(col == 0, 0.0, pltpu.roll(c, 1, 1))
        up = jnp.where(row == nj - 1, high[v : v + 1], pltpu.roll(c, nj - 1, 0))
        down = jnp.where(row == 0, low[v : v + 1], pltpu.roll(c, 1, 0))
        twice = 2.0 * c
        damping = radius_i * (right + left - twice) + radius_j * (up + down - twice)
        out_ref[0, v] = term[v * nj : (v + 1) * nj] - damping


def local_terms(state, metric_i, metric_j, low, high, deriv_i):
    nt, nv, nj, ni = state.shape
    whole3 = pl.BlockSpec((3, nj, ni), lambda t: (0, 0, 0))
    halo = pl.BlockSpec((1, nv, ni), lambda t: (t, 0, 0))
    per_t = pl.BlockSpec((1, nv, nj, ni), lambda t: (t, 0, 0, 0))
    return pl.pallas_call(
        local_kernel,
        grid=(nt,),
        out_shape=pltpu.HBM((nt, nv, nj, ni), jnp.float32),
        in_specs=[per_t, whole3, whole3, halo, halo, pl.BlockSpec((ni, ni), lambda t: (0, 0))],
        out_specs=per_t,
        scratch_shapes=[pltpu.VMEM((nv * nj, ni), jnp.float32)],
        compiler_params=pltpu.CompilerParams(vmem_limit_bytes=VMEM_LIMIT),
        cost_estimate=pl.CostEstimate(
            flops=2 * nt * nv * nj * ni * ni, bytes_accessed=11_000_000, transcendentals=600_000
        ),
        name="local_terms",
    )(in_hbm(state), in_hbm(metric_i), in_hbm(metric_j), low, high, in_hbm(deriv_i))


def add_kernel(me_ref, partial_hbm, *refs):
    out_ref, partial_ref, taken, part_sems, in_sems = refs[-5:]
    sources = refs[:-5]
    nt, nv = out_ref.shape[:2]
    for t in range(nt):
        pltpu.make_async_copy(partial_hbm.at[t], partial_ref.at[t], part_sems.at[t]).start()
    for k, source in enumerate(sources):
        pltpu.make_async_copy(source, taken.at[k], in_sems.at[k]).start()
    for k, source in enumerate(sources):
        pltpu.make_async_copy(source, taken.at[k], in_sems.at[k]).wait()

    @pl.loop(0, nt)
    def _(t):
        pltpu.make_async_copy(partial_hbm.at[t], partial_ref.at[t], part_sems.at[t]).wait()
        for k in range(len(sources)):
            cols = pl.ds(pl.multiple_of((me_ref[0] ^ k) * LANES, LANES), LANES)
            for v in range(nv):
                total = partial_ref[t, v, :, cols] + taken[k, t, v].astype(jnp.float32)
                out_ref[t, v, :, cols] = total.astype(jnp.bfloat16)


def add_sources(me, partial, sources):
    peers = len(sources)
    hbm = pl.BlockSpec(memory_space=pltpu.HBM)
    return pl.pallas_call(
        add_kernel,
        out_shape=pltpu.VMEM(partial.shape, jnp.bfloat16),
        in_specs=[pl.BlockSpec(memory_space=pltpu.SMEM)] + [hbm] * (peers + 1),
        out_specs=pl.BlockSpec(memory_space=pltpu.VMEM),
        scratch_shapes=[
            pltpu.VMEM(partial.shape, jnp.float32),
            pltpu.VMEM((peers,) + sources[0].shape, jnp.bfloat16),
            pltpu.SemaphoreType.DMA((partial.shape[0],)),
            pltpu.SemaphoreType.DMA((peers,)),
        ],
        compiler_params=pltpu.CompilerParams(vmem_limit_bytes=VMEM_SMALL),
        cost_estimate=pl.CostEstimate(flops=1_000_000, bytes_accessed=8_000_000, transcendentals=0),
        name="add_sources",
    )(me, in_hbm(partial), *[in_hbm(x) for x in sources])


def slope_kernel(order, held_ref, lines_ref, deriv_hbm, out_hbm, rest_ref, out_ref, in_sem, sems):
    half = held_ref.shape[0]
    block = out_ref.shape[1]
    blocks = half // block
    rest = pltpu.make_async_copy(deriv_hbm.at[pl.ds(half, half)], rest_ref, in_sem)
    rest.start()

    def out_copy(source):
        return pltpu.make_async_copy(
            out_ref.at[source], out_hbm.at[order.index(source)], sems.at[source]
        )

    def multiply(deriv_ref, base):
        first = 0
        for count in (6, 6, blocks - 12):
            rows = slice(first * block, (first + count) * block)
            total = jnp.dot(deriv_ref[rows, :], lines_ref[...], preferred_element_type=jnp.float32)
            for c in range(count):
                source = base + first + c
                out_ref[source] = total[c * block : (c + 1) * block].astype(jnp.bfloat16)
                out_copy(source).start()
            first += count

    @pl.loop(0, 3)
    def _(step):
        @pl.when(step == 0)
        def _():
            multiply(held_ref, 0)

        @pl.when(step == 1)
        def _():
            rest.wait()
            multiply(rest_ref, blocks)

        @pl.when(step == 2)
        def _():
            for source in range(2 * blocks):
                out_copy(source).wait()


def slope_lines(held, lines, deriv_j, order):
    size, width = lines.shape
    count = len(order)
    shape = (count, size // count, width)
    vmem = pl.BlockSpec(memory_space=pltpu.VMEM)
    hbm = pl.BlockSpec(memory_space=pltpu.HBM)
    return pl.pallas_call(
        functools.partial(slope_kernel, order),
        out_shape=pltpu.HBM(shape, jnp.bfloat16),
        in_specs=[vmem, vmem, hbm],
        out_specs=hbm,
        scratch_shapes=[
            pltpu.VMEM(held.shape, jnp.bfloat16),
            pltpu.VMEM(shape, jnp.bfloat16),
            pltpu.SemaphoreType.DMA,
            pltpu.SemaphoreType.DMA((count,)),
        ],
        compiler_params=pltpu.CompilerParams(vmem_limit_bytes=VMEM_SMALL),
        cost_estimate=pl.CostEstimate(
            flops=2 * size * size * width, bytes_accessed=7_000_000, transcendentals=0
        ),
        name="slope_lines",
    )(held, lines, in_hbm(deriv_j))


def finish_kernel(order, total_ref, slope_ref, out_hbm, out_ref, sems):
    nt, nv = total_ref.shape[:2]
    blocks = slope_ref.shape[0] // nt

    def one(t):
        for b in range(blocks):
            place = order.index(t * blocks + b)
            cols = slice(b * LANES, (b + 1) * LANES)
            for v in range(nv):
                s = slope_ref[place, :, v * LANES : (v + 1) * LANES].astype(jnp.float32)
                total = total_ref[t, v, :, cols].astype(jnp.float32)
                out_ref[t, v, :, cols] = (total + s).astype(jnp.bfloat16)
        pltpu.make_async_copy(out_ref.at[t], out_hbm.at[t], sems.at[t]).start()

    @pl.loop(0, nt)
    def _(step):
        for t in range(nt):
            pl.when(step == t)(functools.partial(one, t))

    @pl.loop(0, nt)
    def _(t):
        pltpu.make_async_copy(out_ref.at[t], out_hbm.at[t], sems.at[t]).wait()


def finish(total, slope, order):
    nt = total.shape[0]
    vmem = pl.BlockSpec(memory_space=pltpu.VMEM)
    return pl.pallas_call(
        functools.partial(finish_kernel, order),
        out_shape=jax.ShapeDtypeStruct(total.shape, jnp.bfloat16),
        in_specs=[vmem, vmem],
        out_specs=pl.BlockSpec(memory_space=pltpu.HBM),
        scratch_shapes=[
            pltpu.VMEM(total.shape, jnp.bfloat16),
            pltpu.SemaphoreType.DMA((nt,)),
        ],
        compiler_params=pltpu.CompilerParams(vmem_limit_bytes=VMEM_SMALL),
        cost_estimate=pl.CostEstimate(flops=1_000_000, bytes_accessed=5_000_000, transcendentals=0),
        name="finish",
    )(total, slope)


def on_device(state, spectral, deriv_i, deriv_j, metric_i, metric_j):
    nt, nv, nj, ni = state.shape
    count = lax.axis_size("space")
    forward = [(i, i + 1) for i in range(count - 1)]
    backward = [(target, source) for source, target in forward]
    peers = lax.axis_size("tm")
    swaps = [[(i, i ^ k) for i in range(peers)] for k in range(peers)]
    rank = lax.axis_index("tm")
    me = jnp.reshape(rank, (1,)).astype(jnp.int32)
    outgoing = flux_j_blocks(state, metric_j).reshape(count, nj, nv * LANES)
    lines = lax.all_to_all(outgoing, "space", split_axis=0, concat_axis=0, tiled=True)
    first, last, own = pack_blocks(me, state)
    low = lax.ppermute(last, "space", forward)
    high = lax.ppermute(first, "space", backward)
    blocks = own[:1] + [lax.ppermute(own[k], "tm", swaps[k]) for k in range(1, peers)]
    sources, held = source_blocks(me, spectral, deriv_j, blocks)
    sources = sources[:1] + [lax.ppermute(sources[k], "tm", swaps[k]) for k in range(1, peers)]
    slope = slope_lines(held, lines.reshape(count * nj, nv * LANES), deriv_j, ORDER)
    slope, low, high = lax.optimization_barrier((slope, low, high))
    slope = lax.all_to_all(
        slope, "space", split_axis=0, concat_axis=0, tiled=True, axis_index_groups=[list(ORDER)]
    )
    partial = local_terms(state, metric_i, metric_j, low, high, deriv_i)
    total = add_sources(me, partial, sources)
    return finish(total, slope, ORDER)


def solution(mesh):
    return jax.shard_map(
        on_device,
        mesh=mesh,
        in_specs=(
            P("tm", None, "space", None),
            P(),
            P(),
            P(),
            P(None, "space", None),
            P(None, "space", None),
        ),
        out_specs=P("tm", None, "space", None),
        check_vma=False,
    )
```

```python
import functools

import jax
import jax.numpy as jnp
from jax import lax
from jax.experimental import pallas as pl
from jax.experimental.pallas import tpu as pltpu
from jax.sharding import PartitionSpec as P

LANES = 128
ORDER = (16, 25, 18, 31, 29, 20, 0, 4, 10, 7, 14, 17, 22, 28, 15, 12, 13, 27, 1, 24, 6, 19, 8, 9, 21, 23, 5, 26, 11, 30, 2, 3)
VMEM_LIMIT = 28 * 1024 * 1024
VMEM_SMALL = 12 * 1024 * 1024


def primitives(cons, metric):
    rho, mx, my, mz, energy = cons
    ax, ay, az = metric
    inv = 1.0 / rho
    contra = (ax * mx + ay * my + az * mz) * inv
    pressure = 0.4 * (energy - 0.5 * (mx * mx + my * my + mz * mz) * inv)
    return inv, contra, pressure


def flux_of(cons, metric, contra, pressure):
    rho, mx, my, mz, energy = cons
    ax, ay, az = metric
    return (
        rho * contra,
        mx * contra + ax * pressure,
        my * contra + ay * pressure,
        mz * contra + az * pressure,
        (energy + pressure) * contra,
    )


def radius_of(metric, inv, contra, pressure):
    ax, ay, az = metric
    return jnp.abs(contra) + jnp.sqrt(1.4 * pressure * inv * (ax * ax + ay * ay + az * az))


def flux_j_kernel(state_hbm, metric_hbm, out_hbm, state_ref, metric_ref, out_ref, in_sems, out_sems):
    nt = state_ref.shape[0]
    blocks = out_ref.shape[1]
    metric_copy = pltpu.make_async_copy(metric_hbm, metric_ref, in_sems.at[nt])
    metric_copy.start()
    copies = [
        pltpu.make_async_copy(state_hbm.at[t], state_ref.at[t], in_sems.at[t]) for t in range(nt)
    ]
    for copy in copies:
        copy.start()
    metric_copy.wait()

    @pl.loop(0, nt)
    def _(t):
        pltpu.make_async_copy(state_hbm.at[t], state_ref.at[t], in_sems.at[t]).wait()
        for b in range(blocks):
            cols = slice(b * LANES, (b + 1) * LANES)
            cons = [state_ref[t, v, :, cols].astype(jnp.float32) for v in range(5)]
            metric = [metric_ref[c, :, cols] for c in range(3)]
            _, contra, pressure = primitives(cons, metric)
            for v, f in enumerate(flux_of(cons, metric, contra, pressure)):
                out_ref[t, b, :, v * LANES : (v + 1) * LANES] = f.astype(jnp.bfloat16)
        pltpu.make_async_copy(out_ref.at[t], out_hbm.at[t], out_sems.at[t]).start()

    @pl.loop(0, nt)
    def _(t):
        pltpu.make_async_copy(out_ref.at[t], out_hbm.at[t], out_sems.at[t]).wait()


def in_hbm(x):
    return pltpu.with_memory_space_constraint(x, pltpu.HBM)


def flux_j_blocks(state, metric_j):
    nt, nv, nj, ni = state.shape
    blocks = ni // LANES
    hbm = pl.BlockSpec(memory_space=pltpu.HBM)
    shape = (nt, blocks, nj, nv * LANES)
    return pl.pallas_call(
        flux_j_kernel,
        out_shape=pltpu.HBM(shape, jnp.bfloat16),
        in_specs=[hbm, hbm],
        out_specs=hbm,
        scratch_shapes=[
            pltpu.VMEM(state.shape, jnp.bfloat16),
            pltpu.VMEM(metric_j.shape, jnp.float32),
            pltpu.VMEM(shape, jnp.bfloat16),
            pltpu.SemaphoreType.DMA((nt + 1,)),
            pltpu.SemaphoreType.DMA((nt,)),
        ],
        compiler_params=pltpu.CompilerParams(vmem_limit_bytes=VMEM_LIMIT),
        cost_estimate=pl.CostEstimate(flops=10_000_000, bytes_accessed=4_000_000, transcendentals=200_000),
        name="flux_j",
    )(in_hbm(state), in_hbm(metric_j))


def pack_kernel(me_ref, state_hbm, *refs):
    state_ref, out_ref, edge_ref, in_sems, out_sems, edge_sems = refs[-6:]
    edges, outs = refs[:2], refs[2:-6]
    nt, nv, nj = state_ref.shape[:3]
    for t in range(nt):
        pltpu.make_async_copy(state_hbm.at[t], state_ref.at[t], in_sems.at[t]).start()

    @pl.loop(0, nt)
    def _(t):
        pltpu.make_async_copy(state_hbm.at[t], state_ref.at[t], in_sems.at[t]).wait()
        for k, out in enumerate(outs):
            cols = pl.ds(pl.multiple_of((me_ref[0] ^ k) * LANES, LANES), LANES)
            for v in range(nv):
                out_ref[k, t, v] = state_ref[t, v, :, cols]
            pltpu.make_async_copy(out_ref.at[k, t], out.at[t], out_sems.at[k, t]).start()
        cons = [state_ref[t, v].astype(jnp.float32) for v in range(nv)]
        for e, row in enumerate((0, nj - 1)):
            rows = jnp.concatenate([c[row : row + 1] for c in cons], axis=0)
            edge_ref[e, t] = rows.astype(jnp.bfloat16)
            pltpu.make_async_copy(edge_ref.at[e, t], edges[e].at[t], edge_sems.at[e, t]).start()

    @pl.loop(0, nt)
    def _(t):
        for k, out in enumerate(outs):
            pltpu.make_async_copy(out_ref.at[k, t], out.at[t], out_sems.at[k, t]).wait()
        for e, edge in enumerate(edges):
            pltpu.make_async_copy(edge_ref.at[e, t], edge.at[t], edge_sems.at[e, t]).wait()


def pack_blocks(me, state):
    nt, nv, nj, ni = state.shape
    peers = ni // LANES
    hbm = pl.BlockSpec(memory_space=pltpu.HBM)
    block = (nt, nv, nj, LANES)
    edge = (nt, nv, ni)
    first, last, *blocks = pl.pallas_call(
        pack_kernel,
        out_shape=[pltpu.HBM(edge, state.dtype)] * 2 + [pltpu.HBM(block, state.dtype)] * peers,
        in_specs=[pl.BlockSpec(memory_space=pltpu.SMEM), hbm],
        out_specs=[hbm] * (peers + 2),
        scratch_shapes=[
            pltpu.VMEM(state.shape, state.dtype),
            pltpu.VMEM((peers,) + block, state.dtype),
            pltpu.VMEM((2,) + edge, state.dtype),
            pltpu.SemaphoreType.DMA((nt,)),
            pltpu.SemaphoreType.DMA((peers, nt)),
            pltpu.SemaphoreType.DMA((2, nt)),
        ],
        compiler_params=pltpu.CompilerParams(vmem_limit_bytes=VMEM_SMALL),
        cost_estimate=pl.CostEstimate(flops=0, bytes_accessed=3_300_000, transcendentals=0),
        name="pack_blocks",
    )(me, in_hbm(state))
    return first, last, blocks


def source_weights(me, spectral, nt):
    size = spectral.shape[0]
    row = lax.broadcasted_iota(jnp.int32, (size * 8, size), 0)
    col = lax.broadcasted_iota(jnp.int32, (size * 8, size), 1)
    instance = (me ^ (row // (nt * 8))) * nt + (row // 8) % nt
    pick = jnp.where(instance == col, 1.0, 0.0).astype(jnp.bfloat16)
    rows = jnp.dot(pick, spectral, preferred_element_type=jnp.float32).astype(jnp.bfloat16)
    full = lax.dot_general(
        rows, pick, (((1,), (1,)), ((), ())), preferred_element_type=jnp.float32
    )
    r = lax.broadcasted_iota(jnp.int32, full.shape, 0)
    c = lax.broadcasted_iota(jnp.int32, full.shape, 1)
    return jnp.where(r % 8 == c % 8, full, 0.0).astype(jnp.bfloat16)


def source_kernel(me_ref, spectral_ref, deriv_hbm, *refs):
    taken, made, stage, result, in_sems, out_sems, sem = refs[-7:]
    peers = taken.shape[0]
    ins, outs, held = refs[:peers], refs[peers : 2 * peers], refs[2 * peers]
    fetches = [pltpu.make_async_copy(ins[k], taken.at[k], in_sems.at[k]) for k in range(peers)]
    for copy in fetches:
        copy.start()
    fetch = pltpu.make_async_copy(deriv_hbm.at[pl.ds(0, held.shape[0])], held, sem)
    fetch.start()
    nt, nv, nj = taken.shape[1:4]
    tiles = nj // 8
    weights = source_weights(me_ref[0], spectral_ref[...], nt)
    for k in range(peers):
        fetches[k].wait()
        for t in range(nt):
            m = k * nt + t
            for v in range(nv):
                x = taken[k, t, v].astype(jnp.float32)
                for b in range(tiles):
                    stage[b, m * 8 : (m + 1) * 8, v * LANES : (v + 1) * LANES] = x[b * 8 : (b + 1) * 8]
    for b in range(tiles):
        result[b] = jnp.dot(
            weights, stage[b].astype(jnp.bfloat16), preferred_element_type=jnp.float32
        )
    sent = []
    for k in range(peers):
        for t in range(nt):
            n = k * nt + t
            for v in range(nv):
                parts = [
                    result[b, n * 8 : (n + 1) * 8, v * LANES : (v + 1) * LANES] for b in range(tiles)
                ]
                made[k, t, v] = jnp.concatenate(parts, axis=0).astype(jnp.bfloat16)
        copy = pltpu.make_async_copy(made.at[k], outs[k], out_sems.at[k])
        copy.start()
        sent.append(copy)
    for copy in sent:
        copy.wait()
    fetch.wait()


def source_blocks(me, spectral, deriv_j, blocks):
    shape = blocks[0].shape
    nt, nv, nj, _ = shape
    peers = len(blocks)
    rows = peers * nt * 8
    vmem = pl.BlockSpec(memory_space=pltpu.VMEM)
    hbm = pl.BlockSpec(memory_space=pltpu.HBM)
    *sources, held = pl.pallas_call(
        source_kernel,
        out_shape=[pltpu.HBM(shape, jnp.bfloat16)] * peers
        + [pltpu.VMEM((deriv_j.shape[0] // 2, deriv_j.shape[1]), deriv_j.dtype)],
        in_specs=[pl.BlockSpec(memory_space=pltpu.SMEM), vmem, hbm] + [hbm] * peers,
        out_specs=[hbm] * peers + [vmem],
        scratch_shapes=[pltpu.VMEM((peers,) + shape, jnp.bfloat16)] * 2
        + [pltpu.VMEM((nj // 8, rows, nv * LANES), jnp.float32)] * 2
        + [pltpu.SemaphoreType.DMA((peers,))] * 2
        + [pltpu.SemaphoreType.DMA],
        compiler_params=pltpu.CompilerParams(vmem_limit_bytes=VMEM_LIMIT),
        cost_estimate=pl.CostEstimate(flops=420_000_000, bytes_accessed=10_000_000, transcendentals=0),
        name="source_blocks",
    )(me, spectral, in_hbm(deriv_j), *[in_hbm(b) for b in blocks])
    return sources, held


def local_kernel(
    state_ref, metric_i_ref, metric_j_ref, low_ref, high_ref, deriv_ref, out_ref, flux_ref
):
    nv, nj, ni = state_ref.shape[1:]
    metric_i = [metric_i_ref[c] for c in range(3)]
    cons = [state_ref[0, v].astype(jnp.float32) for v in range(nv)]
    inv, contra, pressure = primitives(cons, metric_i)
    for v, f in enumerate(flux_of(cons, metric_i, contra, pressure)):
        flux_ref[v * nj : (v + 1) * nj, :] = f
    radius_i = 0.25 * radius_of(metric_i, inv, contra, pressure)
    metric_j = [metric_j_ref[c] for c in range(3)]
    inv, contra, pressure = primitives(cons, metric_j)
    radius_j = 0.25 * radius_of(metric_j, inv, contra, pressure)
    term = lax.dot_general(
        flux_ref[...].astype(jnp.bfloat16),
        deriv_ref[...],
        (((1,), (1,)), ((), ())),
        preferred_element_type=jnp.float32,
    )
    row = lax.broadcasted_iota(jnp.int32, (nj, ni), 0)
    col = lax.broadcasted_iota(jnp.int32, (nj, ni), 1)
    low = low_ref[0].astype(jnp.float32)
    high = high_ref[0].astype(jnp.float32)
    for v in range(nv):
        c = cons[v]
        right = jnp.where(col == ni - 1, 0.0, pltpu.roll(c, ni - 1, 1))
        left = jnp.where(col == 0, 0.0, pltpu.roll(c, 1, 1))
        up = jnp.where(row == nj - 1, high[v : v + 1], pltpu.roll(c, nj - 1, 0))
        down = jnp.where(row == 0, low[v : v + 1], pltpu.roll(c, 1, 0))
        twice = 2.0 * c
        damping = radius_i * (right + left - twice) + radius_j * (up + down - twice)
        out_ref[0, v] = term[v * nj : (v + 1) * nj] - damping


def local_terms(state, metric_i, metric_j, low, high, deriv_i):
    nt, nv, nj, ni = state.shape
    whole3 = pl.BlockSpec((3, nj, ni), lambda t: (0, 0, 0))
    halo = pl.BlockSpec((1, nv, ni), lambda t: (t, 0, 0))
    per_t = pl.BlockSpec((1, nv, nj, ni), lambda t: (t, 0, 0, 0))
    return pl.pallas_call(
        local_kernel,
        grid=(nt,),
        out_shape=pltpu.HBM((nt, nv, nj, ni), jnp.float32),
        in_specs=[per_t, whole3, whole3, halo, halo, pl.BlockSpec((ni, ni), lambda t: (0, 0))],
        out_specs=per_t,
        scratch_shapes=[pltpu.VMEM((nv * nj, ni), jnp.float32)],
        compiler_params=pltpu.CompilerParams(vmem_limit_bytes=VMEM_LIMIT),
        cost_estimate=pl.CostEstimate(
            flops=2 * nt * nv * nj * ni * ni, bytes_accessed=11_000_000, transcendentals=600_000
        ),
        name="local_terms",
    )(in_hbm(state), in_hbm(metric_i), in_hbm(metric_j), low, high, in_hbm(deriv_i))


def add_kernel(me_ref, partial_hbm, *refs):
    out_ref, partial_ref, taken, part_sems, in_sems = refs[-5:]
    sources = refs[:-5]
    nt, nv = out_ref.shape[:2]
    for t in range(nt):
        pltpu.make_async_copy(partial_hbm.at[t], partial_ref.at[t], part_sems.at[t]).start()
    for k, source in enumerate(sources):
        pltpu.make_async_copy(source, taken.at[k], in_sems.at[k]).start()
    for k, source in enumerate(sources):
        pltpu.make_async_copy(source, taken.at[k], in_sems.at[k]).wait()

    @pl.loop(0, nt)
    def _(t):
        pltpu.make_async_copy(partial_hbm.at[t], partial_ref.at[t], part_sems.at[t]).wait()
        for k in range(len(sources)):
            cols = pl.ds(pl.multiple_of((me_ref[0] ^ k) * LANES, LANES), LANES)
            for v in range(nv):
                total = partial_ref[t, v, :, cols] + taken[k, t, v].astype(jnp.float32)
                out_ref[t, v, :, cols] = total.astype(jnp.bfloat16)


def add_sources(me, partial, sources):
    peers = len(sources)
    hbm = pl.BlockSpec(memory_space=pltpu.HBM)
    return pl.pallas_call(
        add_kernel,
        out_shape=pltpu.VMEM(partial.shape, jnp.bfloat16),
        in_specs=[pl.BlockSpec(memory_space=pltpu.SMEM)] + [hbm] * (peers + 1),
        out_specs=pl.BlockSpec(memory_space=pltpu.VMEM),
        scratch_shapes=[
            pltpu.VMEM(partial.shape, jnp.float32),
            pltpu.VMEM((peers,) + sources[0].shape, jnp.bfloat16),
            pltpu.SemaphoreType.DMA((partial.shape[0],)),
            pltpu.SemaphoreType.DMA((peers,)),
        ],
        compiler_params=pltpu.CompilerParams(vmem_limit_bytes=VMEM_SMALL),
        cost_estimate=pl.CostEstimate(flops=1_000_000, bytes_accessed=8_000_000, transcendentals=0),
        name="add_sources",
    )(me, in_hbm(partial), *[in_hbm(x) for x in sources])


def slope_kernel(order, held_ref, lines_ref, deriv_hbm, out_hbm, rest_ref, out_ref, in_sem, sems):
    half = held_ref.shape[0]
    block = out_ref.shape[1]
    blocks = half // block
    rest = pltpu.make_async_copy(deriv_hbm.at[pl.ds(half, half)], rest_ref, in_sem)
    rest.start()

    def out_copy(source):
        return pltpu.make_async_copy(
            out_ref.at[source], out_hbm.at[order.index(source)], sems.at[source]
        )

    def multiply(deriv_ref, base):
        first = 0
        for count in (blocks // 2, blocks // 2):
            rows = slice(first * block, (first + count) * block)
            total = jnp.dot(deriv_ref[rows, :], lines_ref[...], preferred_element_type=jnp.float32)
            for c in range(count):
                source = base + first + c
                out_ref[source] = total[c * block : (c + 1) * block].astype(jnp.bfloat16)
                out_copy(source).start()
            first += count

    @pl.loop(0, 3)
    def _(step):
        @pl.when(step == 0)
        def _():
            multiply(held_ref, 0)

        @pl.when(step == 1)
        def _():
            rest.wait()
            multiply(rest_ref, blocks)

        @pl.when(step == 2)
        def _():
            for source in range(2 * blocks):
                out_copy(source).wait()


def slope_lines(held, lines, deriv_j, order):
    size, width = lines.shape
    count = len(order)
    shape = (count, size // count, width)
    vmem = pl.BlockSpec(memory_space=pltpu.VMEM)
    hbm = pl.BlockSpec(memory_space=pltpu.HBM)
    return pl.pallas_call(
        functools.partial(slope_kernel, order),
        out_shape=pltpu.HBM(shape, jnp.bfloat16),
        in_specs=[vmem, vmem, hbm],
        out_specs=hbm,
        scratch_shapes=[
            pltpu.VMEM(held.shape, jnp.bfloat16),
            pltpu.VMEM(shape, jnp.bfloat16),
            pltpu.SemaphoreType.DMA,
            pltpu.SemaphoreType.DMA((count,)),
        ],
        compiler_params=pltpu.CompilerParams(vmem_limit_bytes=VMEM_SMALL),
        cost_estimate=pl.CostEstimate(
            flops=2 * size * size * width, bytes_accessed=7_000_000, transcendentals=0
        ),
        name="slope_lines",
    )(held, lines, in_hbm(deriv_j))


def finish_kernel(order, total_ref, slope_ref, out_hbm, out_ref, sems):
    nt, nv = total_ref.shape[:2]
    blocks = slope_ref.shape[0] // nt

    def one(t):
        for b in range(blocks):
            place = order.index(t * blocks + b)
            cols = slice(b * LANES, (b + 1) * LANES)
            for v in range(nv):
                s = slope_ref[place, :, v * LANES : (v + 1) * LANES].astype(jnp.float32)
                total = total_ref[t, v, :, cols].astype(jnp.float32)
                out_ref[t, v, :, cols] = (total + s).astype(jnp.bfloat16)
        pltpu.make_async_copy(out_ref.at[t], out_hbm.at[t], sems.at[t]).start()

    @pl.loop(0, nt)
    def _(step):
        for t in range(nt):
            pl.when(step == t)(functools.partial(one, t))

    @pl.loop(0, nt)
    def _(t):
        pltpu.make_async_copy(out_ref.at[t], out_hbm.at[t], sems.at[t]).wait()


def finish(total, slope, order):
    nt = total.shape[0]
    vmem = pl.BlockSpec(memory_space=pltpu.VMEM)
    return pl.pallas_call(
        functools.partial(finish_kernel, order),
        out_shape=jax.ShapeDtypeStruct(total.shape, jnp.bfloat16),
        in_specs=[vmem, vmem],
        out_specs=pl.BlockSpec(memory_space=pltpu.HBM),
        scratch_shapes=[
            pltpu.VMEM(total.shape, jnp.bfloat16),
            pltpu.SemaphoreType.DMA((nt,)),
        ],
        compiler_params=pltpu.CompilerParams(vmem_limit_bytes=VMEM_SMALL),
        cost_estimate=pl.CostEstimate(flops=1_000_000, bytes_accessed=5_000_000, transcendentals=0),
        name="finish",
    )(total, slope)


def on_device(state, spectral, deriv_i, deriv_j, metric_i, metric_j):
    nt, nv, nj, ni = state.shape
    count = lax.axis_size("space")
    forward = [(i, i + 1) for i in range(count - 1)]
    backward = [(target, source) for source, target in forward]
    peers = lax.axis_size("tm")
    swaps = [[(i, i ^ k) for i in range(peers)] for k in range(peers)]
    rank = lax.axis_index("tm")
    me = jnp.reshape(rank, (1,)).astype(jnp.int32)
    outgoing = flux_j_blocks(state, metric_j).reshape(count, nj, nv * LANES)
    lines = lax.all_to_all(outgoing, "space", split_axis=0, concat_axis=0, tiled=True)
    first, last, own = pack_blocks(me, state)
    low = lax.ppermute(last, "space", forward)
    high = lax.ppermute(first, "space", backward)
    blocks = own[:1] + [lax.ppermute(own[k], "tm", swaps[k]) for k in range(1, peers)]
    sources, held = source_blocks(me, spectral, deriv_j, blocks)
    sources = sources[:1] + [lax.ppermute(sources[k], "tm", swaps[k]) for k in range(1, peers)]
    slope = slope_lines(held, lines.reshape(count * nj, nv * LANES), deriv_j, ORDER)
    slope, low, high = lax.optimization_barrier((slope, low, high))
    slope = lax.all_to_all(
        slope, "space", split_axis=0, concat_axis=0, tiled=True, axis_index_groups=[list(ORDER)]
    )
    partial = local_terms(state, metric_i, metric_j, low, high, deriv_i)
    total = add_sources(me, partial, sources)
    return finish(total, slope, ORDER)


def solution(mesh):
    return jax.shard_map(
        on_device,
        mesh=mesh,
        in_specs=(
            P("tm", None, "space", None),
            P(),
            P(),
            P(),
            P(None, "space", None),
            P(None, "space", None),
        ),
        out_specs=P("tm", None, "space", None),
        check_vma=False,
    )
```

```python
import functools

import jax
import jax.numpy as jnp
from jax import lax
from jax.experimental import pallas as pl
from jax.experimental.pallas import tpu as pltpu
from jax.sharding import PartitionSpec as P

LANES = 128
ORDER = (16, 25, 18, 31, 29, 20, 0, 4, 10, 7, 14, 17, 22, 28, 15, 12, 13, 27, 1, 24, 6, 19, 8, 9, 21, 23, 5, 26, 11, 30, 2, 3)
VMEM_LIMIT = 28 * 1024 * 1024
VMEM_SMALL = 12 * 1024 * 1024


def primitives(cons, metric):
    rho, mx, my, mz, energy = cons
    ax, ay, az = metric
    inv = 1.0 / rho
    contra = (ax * mx + ay * my + az * mz) * inv
    pressure = 0.4 * (energy - 0.5 * (mx * mx + my * my + mz * mz) * inv)
    return inv, contra, pressure


def flux_of(cons, metric, contra, pressure):
    rho, mx, my, mz, energy = cons
    ax, ay, az = metric
    return (
        rho * contra,
        mx * contra + ax * pressure,
        my * contra + ay * pressure,
        mz * contra + az * pressure,
        (energy + pressure) * contra,
    )


def radius_of(metric, inv, contra, pressure):
    ax, ay, az = metric
    return jnp.abs(contra) + jnp.sqrt(1.4 * pressure * inv * (ax * ax + ay * ay + az * az))


def flux_j_kernel(state_hbm, metric_hbm, out_hbm, state_ref, metric_ref, out_ref, in_sems, out_sems):
    nt = state_ref.shape[0]
    blocks = out_ref.shape[1]
    metric_copy = pltpu.make_async_copy(metric_hbm, metric_ref, in_sems.at[nt])
    metric_copy.start()
    copies = [
        pltpu.make_async_copy(state_hbm.at[t], state_ref.at[t], in_sems.at[t]) for t in range(nt)
    ]
    for copy in copies:
        copy.start()
    metric_copy.wait()

    @pl.loop(0, nt)
    def _(t):
        pltpu.make_async_copy(state_hbm.at[t], state_ref.at[t], in_sems.at[t]).wait()
        for b in range(blocks):
            cols = slice(b * LANES, (b + 1) * LANES)
            cons = [state_ref[t, v, :, cols].astype(jnp.float32) for v in range(5)]
            metric = [metric_ref[c, :, cols] for c in range(3)]
            _, contra, pressure = primitives(cons, metric)
            for v, f in enumerate(flux_of(cons, metric, contra, pressure)):
                out_ref[t, b, :, v * LANES : (v + 1) * LANES] = f.astype(jnp.bfloat16)
        pltpu.make_async_copy(out_ref.at[t], out_hbm.at[t], out_sems.at[t]).start()

    @pl.loop(0, nt)
    def _(t):
        pltpu.make_async_copy(out_ref.at[t], out_hbm.at[t], out_sems.at[t]).wait()


def in_hbm(x):
    return pltpu.with_memory_space_constraint(x, pltpu.HBM)


def flux_j_blocks(state, metric_j):
    nt, nv, nj, ni = state.shape
    blocks = ni // LANES
    hbm = pl.BlockSpec(memory_space=pltpu.HBM)
    shape = (nt, blocks, nj, nv * LANES)
    return pl.pallas_call(
        flux_j_kernel,
        out_shape=pltpu.HBM(shape, jnp.bfloat16),
        in_specs=[hbm, hbm],
        out_specs=hbm,
        scratch_shapes=[
            pltpu.VMEM(state.shape, jnp.bfloat16),
            pltpu.VMEM(metric_j.shape, jnp.float32),
            pltpu.VMEM(shape, jnp.bfloat16),
            pltpu.SemaphoreType.DMA((nt + 1,)),
            pltpu.SemaphoreType.DMA((nt,)),
        ],
        compiler_params=pltpu.CompilerParams(vmem_limit_bytes=VMEM_LIMIT),
        cost_estimate=pl.CostEstimate(flops=10_000_000, bytes_accessed=4_000_000, transcendentals=200_000),
        name="flux_j",
    )(in_hbm(state), in_hbm(metric_j))


def pack_kernel(me_ref, state_hbm, *refs):
    state_ref, out_ref, edge_ref, in_sems, out_sems, edge_sems = refs[-6:]
    edges, outs = refs[:2], refs[2:-6]
    nt, nv, nj = state_ref.shape[:3]
    for t in range(nt):
        pltpu.make_async_copy(state_hbm.at[t], state_ref.at[t], in_sems.at[t]).start()

    @pl.loop(0, nt)
    def _(t):
        pltpu.make_async_copy(state_hbm.at[t], state_ref.at[t], in_sems.at[t]).wait()
        for k, out in enumerate(outs):
            cols = pl.ds(pl.multiple_of((me_ref[0] ^ k) * LANES, LANES), LANES)
            for v in range(nv):
                out_ref[k, t, v] = state_ref[t, v, :, cols]
            pltpu.make_async_copy(out_ref.at[k, t], out.at[t], out_sems.at[k, t]).start()
        cons = [state_ref[t, v].astype(jnp.float32) for v in range(nv)]
        for e, row in enumerate((0, nj - 1)):
            rows = jnp.concatenate([c[row : row + 1] for c in cons], axis=0)
            edge_ref[e, t] = rows.astype(jnp.bfloat16)
            pltpu.make_async_copy(edge_ref.at[e, t], edges[e].at[t], edge_sems.at[e, t]).start()

    @pl.loop(0, nt)
    def _(t):
        for k, out in enumerate(outs):
            pltpu.make_async_copy(out_ref.at[k, t], out.at[t], out_sems.at[k, t]).wait()
        for e, edge in enumerate(edges):
            pltpu.make_async_copy(edge_ref.at[e, t], edge.at[t], edge_sems.at[e, t]).wait()


def pack_blocks(me, state):
    nt, nv, nj, ni = state.shape
    peers = ni // LANES
    hbm = pl.BlockSpec(memory_space=pltpu.HBM)
    block = (nt, nv, nj, LANES)
    edge = (nt, nv, ni)
    first, last, *blocks = pl.pallas_call(
        pack_kernel,
        out_shape=[pltpu.HBM(edge, state.dtype)] * 2 + [pltpu.HBM(block, state.dtype)] * peers,
        in_specs=[pl.BlockSpec(memory_space=pltpu.SMEM), hbm],
        out_specs=[hbm] * (peers + 2),
        scratch_shapes=[
            pltpu.VMEM(state.shape, state.dtype),
            pltpu.VMEM((peers,) + block, state.dtype),
            pltpu.VMEM((2,) + edge, state.dtype),
            pltpu.SemaphoreType.DMA((nt,)),
            pltpu.SemaphoreType.DMA((peers, nt)),
            pltpu.SemaphoreType.DMA((2, nt)),
        ],
        compiler_params=pltpu.CompilerParams(vmem_limit_bytes=VMEM_SMALL),
        cost_estimate=pl.CostEstimate(flops=0, bytes_accessed=3_300_000, transcendentals=0),
        name="pack_blocks",
    )(me, in_hbm(state))
    return first, last, blocks


def source_weights(me, spectral, nt):
    size = spectral.shape[0]
    row = lax.broadcasted_iota(jnp.int32, (size * 8, size), 0)
    col = lax.broadcasted_iota(jnp.int32, (size * 8, size), 1)
    instance = (me ^ (row // (nt * 8))) * nt + (row // 8) % nt
    pick = jnp.where(instance == col, 1.0, 0.0).astype(jnp.bfloat16)
    rows = jnp.dot(pick, spectral, preferred_element_type=jnp.float32).astype(jnp.bfloat16)
    full = lax.dot_general(
        rows, pick, (((1,), (1,)), ((), ())), preferred_element_type=jnp.float32
    )
    r = lax.broadcasted_iota(jnp.int32, full.shape, 0)
    c = lax.broadcasted_iota(jnp.int32, full.shape, 1)
    return jnp.where(r % 8 == c % 8, full, 0.0).astype(jnp.bfloat16)


def source_kernel(me_ref, spectral_ref, deriv_hbm, *refs):
    taken, made, stage, result, in_sems, out_sems, sem = refs[-7:]
    peers = taken.shape[0]
    ins, outs, held = refs[:peers], refs[peers : 2 * peers], refs[2 * peers]
    fetches = [pltpu.make_async_copy(ins[k], taken.at[k], in_sems.at[k]) for k in range(peers)]
    for copy in fetches:
        copy.start()
    fetch = pltpu.make_async_copy(deriv_hbm.at[pl.ds(0, held.shape[0])], held, sem)
    fetch.start()
    nt, nv, nj = taken.shape[1:4]
    tiles = nj // 8
    weights = source_weights(me_ref[0], spectral_ref[...], nt)
    for k in range(peers):
        fetches[k].wait()
        for t in range(nt):
            m = k * nt + t
            for v in range(nv):
                x = taken[k, t, v].astype(jnp.float32)
                for b in range(tiles):
                    stage[b, m * 8 : (m + 1) * 8, v * LANES : (v + 1) * LANES] = x[b * 8 : (b + 1) * 8]
    for b in range(tiles):
        result[b] = jnp.dot(
            weights, stage[b].astype(jnp.bfloat16), preferred_element_type=jnp.float32
        )
    sent = []
    for k in range(peers):
        for t in range(nt):
            n = k * nt + t
            for v in range(nv):
                parts = [
                    result[b, n * 8 : (n + 1) * 8, v * LANES : (v + 1) * LANES] for b in range(tiles)
                ]
                made[k, t, v] = jnp.concatenate(parts, axis=0).astype(jnp.bfloat16)
        copy = pltpu.make_async_copy(made.at[k], outs[k], out_sems.at[k])
        copy.start()
        sent.append(copy)
    for copy in sent:
        copy.wait()
    fetch.wait()


def source_blocks(me, spectral, deriv_j, blocks):
    shape = blocks[0].shape
    nt, nv, nj, _ = shape
    peers = len(blocks)
    rows = peers * nt * 8
    vmem = pl.BlockSpec(memory_space=pltpu.VMEM)
    hbm = pl.BlockSpec(memory_space=pltpu.HBM)
    *sources, held = pl.pallas_call(
        source_kernel,
        out_shape=[pltpu.HBM(shape, jnp.bfloat16)] * peers
        + [pltpu.VMEM((deriv_j.shape[0] // 2, deriv_j.shape[1]), deriv_j.dtype)],
        in_specs=[pl.BlockSpec(memory_space=pltpu.SMEM), vmem, hbm] + [hbm] * peers,
        out_specs=[hbm] * peers + [vmem],
        scratch_shapes=[pltpu.VMEM((peers,) + shape, jnp.bfloat16)] * 2
        + [pltpu.VMEM((nj // 8, rows, nv * LANES), jnp.float32)] * 2
        + [pltpu.SemaphoreType.DMA((peers,))] * 2
        + [pltpu.SemaphoreType.DMA],
        compiler_params=pltpu.CompilerParams(vmem_limit_bytes=VMEM_LIMIT),
        cost_estimate=pl.CostEstimate(flops=420_000_000, bytes_accessed=10_000_000, transcendentals=0),
        name="source_blocks",
    )(me, spectral, in_hbm(deriv_j), *[in_hbm(b) for b in blocks])
    return sources, held


def local_kernel(
    state_ref, metric_i_ref, metric_j_ref, low_ref, high_ref, deriv_ref, out_ref, flux_ref
):
    nv, nj, ni = state_ref.shape[1:]
    metric_i = [metric_i_ref[c] for c in range(3)]
    cons = [state_ref[0, v].astype(jnp.float32) for v in range(nv)]
    inv, contra, pressure = primitives(cons, metric_i)
    for v, f in enumerate(flux_of(cons, metric_i, contra, pressure)):
        flux_ref[v * nj : (v + 1) * nj, :] = f
    radius_i = 0.25 * radius_of(metric_i, inv, contra, pressure)
    metric_j = [metric_j_ref[c] for c in range(3)]
    inv, contra, pressure = primitives(cons, metric_j)
    radius_j = 0.25 * radius_of(metric_j, inv, contra, pressure)
    term = lax.dot_general(
        flux_ref[...].astype(jnp.bfloat16),
        deriv_ref[...],
        (((1,), (1,)), ((), ())),
        preferred_element_type=jnp.float32,
    )
    row = lax.broadcasted_iota(jnp.int32, (nj, ni), 0)
    col = lax.broadcasted_iota(jnp.int32, (nj, ni), 1)
    low = low_ref[0].astype(jnp.float32)
    high = high_ref[0].astype(jnp.float32)
    for v in range(nv):
        c = cons[v]
        right = jnp.where(col == ni - 1, 0.0, pltpu.roll(c, ni - 1, 1))
        left = jnp.where(col == 0, 0.0, pltpu.roll(c, 1, 1))
        up = jnp.where(row == nj - 1, high[v : v + 1], pltpu.roll(c, nj - 1, 0))
        down = jnp.where(row == 0, low[v : v + 1], pltpu.roll(c, 1, 0))
        twice = 2.0 * c
        damping = radius_i * (right + left - twice) + radius_j * (up + down - twice)
        out_ref[0, v] = term[v * nj : (v + 1) * nj] - damping


def local_terms(state, metric_i, metric_j, low, high, deriv_i):
    nt, nv, nj, ni = state.shape
    whole3 = pl.BlockSpec((3, nj, ni), lambda t: (0, 0, 0))
    halo = pl.BlockSpec((1, nv, ni), lambda t: (t, 0, 0))
    per_t = pl.BlockSpec((1, nv, nj, ni), lambda t: (t, 0, 0, 0))
    return pl.pallas_call(
        local_kernel,
        grid=(nt,),
        out_shape=pltpu.HBM((nt, nv, nj, ni), jnp.float32),
        in_specs=[per_t, whole3, whole3, halo, halo, pl.BlockSpec((ni, ni), lambda t: (0, 0))],
        out_specs=per_t,
        scratch_shapes=[pltpu.VMEM((nv * nj, ni), jnp.float32)],
        compiler_params=pltpu.CompilerParams(vmem_limit_bytes=VMEM_LIMIT),
        cost_estimate=pl.CostEstimate(
            flops=2 * nt * nv * nj * ni * ni, bytes_accessed=11_000_000, transcendentals=600_000
        ),
        name="local_terms",
    )(in_hbm(state), in_hbm(metric_i), in_hbm(metric_j), low, high, in_hbm(deriv_i))


def add_kernel(me_ref, partial_hbm, *refs):
    out_ref, partial_ref, taken, part_sems, in_sems = refs[-5:]
    sources = refs[:-5]
    nt, nv = out_ref.shape[:2]
    for t in range(nt):
        pltpu.make_async_copy(partial_hbm.at[t], partial_ref.at[t], part_sems.at[t]).start()
    for k, source in enumerate(sources):
        pltpu.make_async_copy(source, taken.at[k], in_sems.at[k]).start()
    for k, source in enumerate(sources):
        pltpu.make_async_copy(source, taken.at[k], in_sems.at[k]).wait()

    @pl.loop(0, nt)
    def _(t):
        pltpu.make_async_copy(partial_hbm.at[t], partial_ref.at[t], part_sems.at[t]).wait()
        for k in range(len(sources)):
            cols = pl.ds(pl.multiple_of((me_ref[0] ^ k) * LANES, LANES), LANES)
            for v in range(nv):
                total = partial_ref[t, v, :, cols] + taken[k, t, v].astype(jnp.float32)
                out_ref[t, v, :, cols] = total.astype(jnp.bfloat16)


def add_sources(me, partial, sources):
    peers = len(sources)
    hbm = pl.BlockSpec(memory_space=pltpu.HBM)
    return pl.pallas_call(
        add_kernel,
        out_shape=pltpu.VMEM(partial.shape, jnp.bfloat16),
        in_specs=[pl.BlockSpec(memory_space=pltpu.SMEM)] + [hbm] * (peers + 1),
        out_specs=pl.BlockSpec(memory_space=pltpu.VMEM),
        scratch_shapes=[
            pltpu.VMEM(partial.shape, jnp.float32),
            pltpu.VMEM((peers,) + sources[0].shape, jnp.bfloat16),
            pltpu.SemaphoreType.DMA((partial.shape[0],)),
            pltpu.SemaphoreType.DMA((peers,)),
        ],
        compiler_params=pltpu.CompilerParams(vmem_limit_bytes=VMEM_SMALL),
        cost_estimate=pl.CostEstimate(flops=1_000_000, bytes_accessed=8_000_000, transcendentals=0),
        name="add_sources",
    )(me, in_hbm(partial), *[in_hbm(x) for x in sources])


def slope_kernel(order, held_ref, lines_ref, deriv_hbm, out_hbm, rest_ref, out_ref, in_sem, sems):
    half = held_ref.shape[0]
    block = out_ref.shape[1]
    blocks = half // block
    rest = pltpu.make_async_copy(deriv_hbm.at[pl.ds(half, half)], rest_ref, in_sem)
    rest.start()

    def out_copy(source):
        return pltpu.make_async_copy(
            out_ref.at[source], out_hbm.at[order.index(source)], sems.at[source]
        )

    def multiply(deriv_ref, base):
        first = 0
        for count in (blocks - 6, 6):
            rows = slice(first * block, (first + count) * block)
            total = jnp.dot(deriv_ref[rows, :], lines_ref[...], preferred_element_type=jnp.float32)
            for c in range(count):
                source = base + first + c
                out_ref[source] = total[c * block : (c + 1) * block].astype(jnp.bfloat16)
                out_copy(source).start()
            first += count

    @pl.loop(0, 3)
    def _(step):
        @pl.when(step == 0)
        def _():
            multiply(held_ref, 0)

        @pl.when(step == 1)
        def _():
            rest.wait()
            multiply(rest_ref, blocks)

        @pl.when(step == 2)
        def _():
            for source in range(2 * blocks):
                out_copy(source).wait()


def slope_lines(held, lines, deriv_j, order):
    size, width = lines.shape
    count = len(order)
    shape = (count, size // count, width)
    vmem = pl.BlockSpec(memory_space=pltpu.VMEM)
    hbm = pl.BlockSpec(memory_space=pltpu.HBM)
    return pl.pallas_call(
        functools.partial(slope_kernel, order),
        out_shape=pltpu.HBM(shape, jnp.bfloat16),
        in_specs=[vmem, vmem, hbm],
        out_specs=hbm,
        scratch_shapes=[
            pltpu.VMEM(held.shape, jnp.bfloat16),
            pltpu.VMEM(shape, jnp.bfloat16),
            pltpu.SemaphoreType.DMA,
            pltpu.SemaphoreType.DMA((count,)),
        ],
        compiler_params=pltpu.CompilerParams(vmem_limit_bytes=VMEM_SMALL),
        cost_estimate=pl.CostEstimate(
            flops=2 * size * size * width, bytes_accessed=7_000_000, transcendentals=0
        ),
        name="slope_lines",
    )(held, lines, in_hbm(deriv_j))


def finish_kernel(order, total_ref, slope_ref, out_hbm, out_ref, sems):
    nt, nv = total_ref.shape[:2]
    blocks = slope_ref.shape[0] // nt

    def one(t):
        for b in range(blocks):
            place = order.index(t * blocks + b)
            cols = slice(b * LANES, (b + 1) * LANES)
            for v in range(nv):
                s = slope_ref[place, :, v * LANES : (v + 1) * LANES].astype(jnp.float32)
                total = total_ref[t, v, :, cols].astype(jnp.float32)
                out_ref[t, v, :, cols] = (total + s).astype(jnp.bfloat16)
        pltpu.make_async_copy(out_ref.at[t], out_hbm.at[t], sems.at[t]).start()

    @pl.loop(0, nt)
    def _(step):
        for t in range(nt):
            pl.when(step == t)(functools.partial(one, t))

    @pl.loop(0, nt)
    def _(t):
        pltpu.make_async_copy(out_ref.at[t], out_hbm.at[t], sems.at[t]).wait()


def finish(total, slope, order):
    nt = total.shape[0]
    vmem = pl.BlockSpec(memory_space=pltpu.VMEM)
    return pl.pallas_call(
        functools.partial(finish_kernel, order),
        out_shape=jax.ShapeDtypeStruct(total.shape, jnp.bfloat16),
        in_specs=[vmem, vmem],
        out_specs=pl.BlockSpec(memory_space=pltpu.HBM),
        scratch_shapes=[
            pltpu.VMEM(total.shape, jnp.bfloat16),
            pltpu.SemaphoreType.DMA((nt,)),
        ],
        compiler_params=pltpu.CompilerParams(vmem_limit_bytes=VMEM_SMALL),
        cost_estimate=pl.CostEstimate(flops=1_000_000, bytes_accessed=5_000_000, transcendentals=0),
        name="finish",
    )(total, slope)


def on_device(state, spectral, deriv_i, deriv_j, metric_i, metric_j):
    nt, nv, nj, ni = state.shape
    count = lax.axis_size("space")
    forward = [(i, i + 1) for i in range(count - 1)]
    backward = [(target, source) for source, target in forward]
    peers = lax.axis_size("tm")
    swaps = [[(i, i ^ k) for i in range(peers)] for k in range(peers)]
    rank = lax.axis_index("tm")
    me = jnp.reshape(rank, (1,)).astype(jnp.int32)
    outgoing = flux_j_blocks(state, metric_j).reshape(count, nj, nv * LANES)
    lines = lax.all_to_all(outgoing, "space", split_axis=0, concat_axis=0, tiled=True)
    first, last, own = pack_blocks(me, state)
    low = lax.ppermute(last, "space", forward)
    high = lax.ppermute(first, "space", backward)
    blocks = own[:1] + [lax.ppermute(own[k], "tm", swaps[k]) for k in range(1, peers)]
    sources, held = source_blocks(me, spectral, deriv_j, blocks)
    sources = sources[:1] + [lax.ppermute(sources[k], "tm", swaps[k]) for k in range(1, peers)]
    slope = slope_lines(held, lines.reshape(count * nj, nv * LANES), deriv_j, ORDER)
    slope, low, high = lax.optimization_barrier((slope, low, high))
    slope = lax.all_to_all(
        slope, "space", split_axis=0, concat_axis=0, tiled=True, axis_index_groups=[list(ORDER)]
    )
    partial = local_terms(state, metric_i, metric_j, low, high, deriv_i)
    total = add_sources(me, partial, sources)
    return finish(total, slope, ORDER)


def solution(mesh):
    return jax.shard_map(
        on_device,
        mesh=mesh,
        in_specs=(
            P("tm", None, "space", None),
            P(),
            P(),
            P(),
            P(None, "space", None),
            P(None, "space", None),
        ),
        out_specs=P("tm", None, "space", None),
        check_vma=False,
    )
```
